32 devices in a mesh: segment: 4 (over y, x), seq: 4 (over z), mp: 2 (over core).
Axes of the slice: x: 2, y: 2, z: 4, core: 2. Of those that a mesh axis runs over, the one named last changes fastest.
Arguments:
- video: bfloat16 [3, 256, 6144], P(None, 'seq', 'mp'), may hold values from -6 to 6
- caption_kv: bfloat16 [4, 768, 2, 3072], P('segment', 'seq', None, 'mp'), may hold values from -6 to 6
- caption_lengths: int32 [3], replicated, may hold values from 1 to 400, 768 in all
- order: int32 [3], replicated, may hold values from 0 to 2, each once
- gains: float32 [4, 6144], P('segment'), may hold values from 0.25 to 1.75
- w_query: bfloat16 [4, 6144, 3072], P('segment', 'seq', 'mp')
- w_out: bfloat16 [4, 3072, 6144], P('segment', None, 'mp'), may hold values from -0.109375 to 0.109375
Outputs:
- section_out: bfloat16 [4, 3, 256, 6144], P('segment', None, 'seq', 'mp')
The draws below stay inside these ranges and needn't reach their ends.
Inputs may be any that keep to these rules, and one draw needn't show every extreme that they name: `caption_lengths`: caption lengths sum to 768; the largest is exactly 400. `order`: each sample is named by exactly one micro-batch.
All inputs are finite; a program needn't handle non-finite values.
Results may differ from the reference program's by a relative error of at most 0.009.
Values may be sent and summed in bfloat16 or wider, within the bound.
A program may use at most 128 MiB of HBM per device.

```python
import math
import jax
import jax.numpy as jnp
import numpy as np
from jax import lax

D = 6144
HEADS = 24
HEAD_DIM = 128
HW = 3072
L = 256
SAMPLES = 3
CAPROWS = 768
CAPMAX = 400


def draw_video(key, part):
    key = jax.random.fold_in(key, 11)
    base = jnp.clip(jax.random.normal(key, (SAMPLES, L, D), jnp.float32), -6.0, 6.0)
    return base.astype(jnp.bfloat16)


def draw_w_query(key, part):
    key = jax.random.fold_in(key, 12)
    base = jax.random.truncated_normal(key, -6.0, 6.0, (4, D, HW), jnp.float32) * D ** (-0.5)
    return base.astype(jnp.bfloat16)


def draw_caption_kv(key, part):
    key = jax.random.fold_in(key, 13)
    base = jnp.clip(jax.random.normal(key, (4, CAPROWS, 2, HW), jnp.float32), -6.0, 6.0)
    return base.astype(jnp.bfloat16)


def shard_levels(key, shape, shards, least, top_value):
    def one(dim, shards_of):
        draws = jax.random.uniform(jax.random.fold_in(jax.random.fold_in(key, 6), dim), (shards_of,), jnp.float32, least / len(shards), top_value / len(shards))
        return jnp.repeat(jnp.exp(draws), shape[dim] // shards_of).reshape((-1,) + (1,) * (len(shape) - dim - 1))

    level = one(*shards[0])
    for cut in shards[1:]:
        level = level * one(*cut)
    return level


def split_up(number_of, total, most, slope):
    weights = [(1 << 20) // math.isqrt(rank ** slope) + 1 for rank in range(2, number_of + 1)]
    rest, holding = total - most - (number_of - 1), [1] * (number_of - 1)
    while rest > 0:
        free = [i for i in range(number_of - 1) if holding[i] < most]
        mass, remaining = sum([weights[i] for i in free]), rest
        for i in free:
            more = min(most - holding[i], max(1, remaining * weights[i] // mass), rest)
            holding[i] = holding[i] + more
            rest = rest - more
    return np.array([most] + holding)


def ragged(stream_key, count, total, bound, skew):
    if count == 2:
        one = jax.random.randint(stream_key, (), max(1, total - bound), min(bound, total - 1) + 1)
        return jnp.stack([one, total - one])
    sizes = jnp.asarray(split_up(count, total, bound, skew), jnp.int32)
    twos = (count - 1) // 2
    source_of, receiver = sizes[1:1 + 2 * twos:2], sizes[2:2 + 2 * twos:2]
    margin = jnp.minimum(source_of - 1, bound - receiver)
    passed = jax.random.randint(jax.random.fold_in(stream_key, 1), (twos,), 0, 1 << 20) % (margin + 1)
    sizes = sizes.at[1:1 + 2 * twos:2].set(source_of - passed).at[2:2 + 2 * twos:2].set(receiver + passed)
    return sizes[jax.random.permutation(jax.random.fold_in(stream_key, 2), count)]


def centred(stream_key, dims, spread, reach, cuts=(), kind=jnp.bfloat16):
    level = shard_levels(stream_key, dims, cuts, -0.22, 0.18) if cuts else 1.0
    values = jax.random.normal(stream_key, dims, jnp.float32) * spread * level
    return jnp.minimum(jnp.maximum(values, -reach), reach).astype(kind)


def setup_inputs(seed: int = 0) -> dict:
    splits = jax.random.split(jax.random.key(seed), 8)
    return {
        "video": draw_video(jax.random.fold_in(splits[7], 71), 0),
        "caption_kv": draw_caption_kv(jax.random.fold_in(splits[7], 71), 0),
        "caption_lengths": ragged(splits[2], SAMPLES, CAPROWS, CAPMAX, 0).astype(jnp.int32),
        "order": jax.random.permutation(splits[3], SAMPLES).astype(jnp.int32),
        "gains": jnp.clip(1.0 + 0.15 * jax.random.normal(splits[4], (4, D), jnp.float32), 0.25, 1.75),
        "w_query": draw_w_query(jax.random.fold_in(splits[7], 71), 0),
        "w_out": centred(splits[6], (4, HW, D), HW ** -0.5, 0.109375, ((0, 4), (2, 2))),
    }


def section(x, gain, w_query, w_out, kv, valid):
    xf = x.astype(jnp.float32)
    meansq = lax.optimization_barrier(jnp.mean(xf * xf, axis=-1, keepdims=True))
    normed = (xf * lax.rsqrt(meansq + 1e-06) * gain).astype(jnp.bfloat16)
    query = jnp.dot(normed, w_query, preferred_element_type=jnp.float32).astype(jnp.bfloat16)
    rows = query.shape[0]
    qheads = query.astype(jnp.float32).reshape(rows, HEADS, HEAD_DIM)
    keys = kv[:, 0, :].astype(jnp.float32).reshape(CAPROWS, HEADS, HEAD_DIM)
    values = kv[:, 1, :].astype(jnp.float32).reshape(CAPROWS, HEADS, HEAD_DIM)
    scores = jnp.einsum('thd,rhd->htr', qheads, keys) * HEAD_DIM ** (-0.5)
    scores = jnp.where(valid[None, None, :], scores, -1e+30)
    top = lax.optimization_barrier(jnp.max(scores, axis=-1, keepdims=True))
    weights = jnp.where(valid[None, None, :], jnp.exp(scores - top), 0.0)
    total = lax.optimization_barrier(jnp.sum(weights, axis=-1))
    acc = jnp.einsum('htr,rhd->htd', weights, values) / total[:, :, None]
    attended = jnp.transpose(acc, (1, 0, 2)).reshape(rows, HEADS * HEAD_DIM).astype(jnp.bfloat16)
    mixed = xf + jnp.dot(attended, w_out, preferred_element_type=jnp.float32)
    return mixed.astype(jnp.bfloat16)

def reference(video, caption_kv, caption_lengths, order, gains, w_query, w_out):
    offsets = (jnp.cumsum(caption_lengths) - caption_lengths).astype(jnp.int32)
    row_index = jnp.arange(CAPROWS, dtype=jnp.int32)
    results = []
    for micro in range(SAMPLES):
        sample = order[micro]
        current = jnp.take(video, sample, axis=0)
        start_row = offsets[sample]
        valid = (row_index >= start_row) & (row_index < start_row + caption_lengths[sample])
        stacked = []
        for segment_index in range(4):
            current = section(current, gains[segment_index], w_query[segment_index], w_out[segment_index], caption_kv[segment_index], valid)
            stacked.append(current)
        results.append(jnp.stack(stacked))
    return jnp.stack(results, axis=1)
```

```python
import functools
import jax
import jax.numpy as jnp
from jax import lax
from jax.experimental import pallas as pl
from jax.experimental.pallas import tpu as pltpu
from jax.sharding import PartitionSpec as P

HEAD_DIM = 128
SPLIT = 2
MESH = pl.DeviceIdType.MESH


def passed_along(block, axis, distance):
    devices = range(lax.axis_size(axis))
    route = [(i - distance, i) for i in devices if i - distance in devices]
    return lax.ppermute(block, axis, route)


def block_terms(query, kv, start_row, length):
    tokens = query.shape[0]
    heads = query.shape[1] // HEAD_DIM
    count = kv.shape[0]
    qheads = query.reshape(tokens, heads, HEAD_DIM)
    keys = kv[:, 0, :].reshape(count, heads, HEAD_DIM)
    values = kv[:, 1, :].astype(jnp.float32).reshape(count, heads, HEAD_DIM)
    scores = jnp.einsum(
        "thd,rhd->htr", qheads, keys, preferred_element_type=jnp.float32
    ) * HEAD_DIM ** (-0.5)
    rows = jnp.arange(count, dtype=jnp.int32)
    valid = (rows >= start_row) & (rows < start_row + length)
    scores = jnp.where(valid[None, None, :], scores, -1e30)
    top = jnp.max(scores, axis=-1)
    weights = jnp.where(valid[None, None, :], jnp.exp(scores - top[:, :, None]), 0.0)
    total = jnp.sum(weights, axis=-1)
    acc = jnp.einsum("htr,rhd->htd", weights, values)
    return (top, total, acc)


def finish(total, acc):
    heads, tokens, width = acc.shape
    result = acc / total[:, :, None]
    return jnp.transpose(result, (1, 0, 2)).reshape(tokens, heads * width).astype(jnp.bfloat16)


def general(video, caption_kv, caption_lengths, order, gains, w_query, w_out):
    samples = video.shape[0]
    segments = lax.axis_size("segment")
    here = lax.axis_index("segment")
    gain = gains[0]
    w_local = w_query[0]
    out_weight = w_out[0]
    kv_local = caption_kv[0]
    offsets = jnp.cumsum(caption_lengths) - caption_lengths
    w_whole = lax.all_gather(w_local, "seq", axis=0, tiled=True)
    kv_whole = lax.all_gather(kv_local, "seq", axis=0, tiled=True)
    received = jnp.zeros_like(video[0])
    section_out = jnp.zeros_like(video)
    for tick in range(samples + segments - 1):
        micro = tick - here
        active = (micro >= 0) & (micro < samples)
        slot = jnp.clip(micro, 0, samples - 1)
        sample = order[slot]
        first = lax.dynamic_index_in_dim(video, sample, 0, keepdims=False)
        current = jnp.where(here == 0, first, received)
        whole = lax.all_gather(current, "mp", axis=1, tiled=True)
        wholef = whole.astype(jnp.float32)
        meansq = jnp.mean(wholef * wholef, axis=-1, keepdims=True)
        normed = (wholef * lax.rsqrt(meansq + 1e-06) * gain).astype(jnp.bfloat16)
        query = jnp.dot(normed, w_whole, preferred_element_type=jnp.float32)
        query = query.astype(jnp.bfloat16)
        start_row = offsets[sample]
        length = caption_lengths[sample]
        top, total, acc = block_terms(query, kv_whole, start_row, length)
        attended = finish(total, acc)
        projected = jnp.dot(
            lax.all_gather(attended, "mp", axis=1, tiled=True),
            out_weight,
            preferred_element_type=jnp.float32,
        )
        mixed = (current.astype(jnp.float32) + projected).astype(jnp.bfloat16)
        updated = lax.dynamic_update_index_in_dim(section_out, mixed, slot, 0)
        section_out = jnp.where(active, updated, section_out)
        received = passed_along(mixed, "segment", 1)
    return section_out[None]


def relay_kernel(cfg, bounds, x0, gain_ref, kv_ref, wq_ref, wout_ref, out_ref,
                 res, xg, qs, qr, ts, tr, ats, atr, flat, kvb, wqv, woutv,
                 load_sem, kv_send, kv_recv, rel_send, rel_recv, x_send, x_recv, f_send,
                 q_send, q_recv, t_send, t_recv, a_send, a_recv, b_send, b_recv):
    segments, seq, chunks, tl, split = cfg
    blocks = seq // 2
    g = lax.axis_index("segment")
    s = lax.axis_index("seq")
    c = lax.axis_index("mp")
    width = xg.shape[-1]
    cols = qs.shape[-1]
    half = res.shape[-1]
    tokens = seq * tl
    hub = s // blocks == c
    sibling = {"mp": 1 - c}

    def remote(src, dst, send, recv, device):
        return pltpu.make_async_remote_copy(
            src_ref=src, dst_ref=dst, send_sem=send, recv_sem=recv,
            device_id=device, device_id_type=MESH)

    def peers(fn):
        for off in range(1, seq):
            fn(lax.rem(s + off, seq))

    def kv_copy(d):
        return remote(kv_ref.at[d], kvb.at[s], kv_send.at[d], kv_recv.at[s], {"seq": d})

    def kv_arrival(d):
        return remote(kv_ref.at[d], kvb.at[d], kv_send.at[d], kv_recv.at[d], {"seq": d})

    def rel_copy(k, j):
        part = pl.ds(j * width, width)
        return remote(out_ref.at[k, :, part], res.at[k, :, part],
                      rel_send.at[k, j], rel_recv.at[k, j], {"segment": g + 1})

    def x_copy(k, j):
        part = pl.ds(j * width, width)
        return remote(res.at[k, :, part], xg.at[k, s], x_send.at[k, j], x_recv.at[k, s],
                      {"seq": blocks * c + j})

    def forward_copy(k, d):
        return remote(xg.at[k, d], xg.at[k, d], f_send.at[k, d], x_recv.at[k, d], sibling)

    def q_copy(k, d):
        return remote(qs.at[k, d], qr.at[k, s], q_send.at[k, d], q_recv.at[k, s], {"seq": d})

    def q_arrival(k, d):
        return remote(qs.at[k, d], qr.at[k, d], q_send.at[k, d], q_recv.at[k, d], {"seq": d})

    def t_copy(k, d):
        return remote(ts.at[k], tr.at[k, s], t_send.at[k, d], t_recv.at[k, s], {"seq": d})

    def t_arrival(k, d):
        return remote(ts.at[k], tr.at[k, d], t_send.at[k, d], t_recv.at[k, d], {"seq": d})

    def a_copy(k, d):
        return remote(ats.at[k, d], atr.at[k, c, s], a_send.at[k, d], a_recv.at[k, s], {"seq": d})

    def a_arrival(k, d):
        return remote(ats.at[k, d], atr.at[k, c, d], a_send.at[k, d], a_recv.at[k, d], {"seq": d})

    def b_copy(k, d):
        return remote(atr.at[k, c, d], atr.at[k, c, d], b_send.at[k, d], b_recv.at[k, d], sibling)

    def b_arrival(k, d):
        return remote(atr.at[k, 1 - c, d], atr.at[k, 1 - c, d], b_send.at[k, d], b_recv.at[k, d], sibling)

    load_wq = pltpu.make_async_copy(wq_ref, wqv, load_sem.at[0])
    load_wout = pltpu.make_async_copy(wout_ref, woutv, load_sem.at[1])
    load_kv = pltpu.make_async_copy(kv_ref.at[s], kvb.at[s], load_sem.at[2])
    load_x = pltpu.make_async_copy(x0, res, load_sem.at[3])

    @pl.when(g == 0)
    def _():
        load_x.start()

    load_wq.start()
    load_kv.start()
    load_wout.start()

    barrier = pltpu.get_barrier_semaphore()

    def greet(device):
        pl.semaphore_signal(barrier, inc=1, device_id=device, device_id_type=MESH)

    peers(lambda d: greet({"seq": d}))
    greet(sibling)

    @pl.when(g > 0)
    def _():
        greet({"segment": g - 1})

    @pl.when(g < segments - 1)
    def _():
        greet({"segment": g + 1})

    inner = (g > 0) & (g < segments - 1)

    @pl.when(inner)
    def _():
        pl.semaphore_wait(barrier, seq + 2)

    @pl.when(jnp.logical_not(inner))
    def _():
        pl.semaphore_wait(barrier, seq + 1)

    @pl.when(g == 0)
    def _():
        load_x.wait()

    def send_x(k):
        for j in range(blocks):
            @pl.when(g > 0)
            def _():
                remote(out_ref.at[k, :, pl.ds(j * width, width)], res.at[k, :, pl.ds(j * width, width)],
                       rel_send.at[k, j], rel_recv.at[k, j], {"segment": g - 1}).wait_recv()

            mine = blocks * c + j == s

            @pl.when(mine)
            def _():
                xg[k, s] = res[k, :, j * width:(j + 1) * width]
                forward_copy(k, s).start()

            @pl.when(jnp.logical_not(mine))
            def _():
                x_copy(k, j).start()

    def collect_x(k):
        @pl.when(hub)
        def _():
            def one(d):
                forward_copy(k, d).wait_recv()
                forward_copy(k, d).start()
            peers(one)

        @pl.when(jnp.logical_not(hub))
        def _():
            for d in range(seq):
                forward_copy(k, d).wait_recv()

    def project(k):
        x = xg[k].reshape(tokens, width).astype(jnp.float32)
        square = jnp.sum(x * x, axis=-1, keepdims=True)
        ts[k] = jnp.transpose(jnp.broadcast_to(square, (tokens, 128)))[:8]
        y = (x * gain_ref[:, pl.ds(pl.multiple_of(s * width, width), width)]).astype(jnp.bfloat16)

        def one(d):
            t_copy(k, d).start()
            w = wqv[:, pl.ds(pl.multiple_of(d * cols, cols), cols)]
            qs[k, d] = jnp.dot(y, w, preferred_element_type=jnp.float32).astype(jnp.bfloat16)
            q_copy(k, d).start()
        peers(one)
        w = wqv[:, pl.ds(pl.multiple_of(s * cols, cols), cols)]
        qr[k, s] = jnp.dot(y, w, preferred_element_type=jnp.float32).astype(jnp.bfloat16)
        tr[k, s] = ts[k]

    def attend(k):
        def arrived(d):
            t_arrival(k, d).wait_recv()
            q_arrival(k, d).wait_recv()
        peers(arrived)
        square = jnp.sum(tr[k], axis=0)[:1]
        square = jnp.transpose(jnp.broadcast_to(square, (128, tokens)))
        scale = lax.rsqrt(square / (seq * width) + 1e-6)
        total = qr[k, 0].astype(jnp.float32)
        for d in range(1, seq):
            total = total + qr[k, d].astype(jnp.float32)
        micro = k // split
        first, last = bounds[0, micro], bounds[1, micro]
        rows = kvb.shape[2] * seq
        index = lax.broadcasted_iota(jnp.int32, (1, rows), 1)
        valid = (index >= first) & (index < last)
        for h in range(cols // HEAD_DIM):
            part = slice(h * HEAD_DIM, (h + 1) * HEAD_DIM)
            q = (total[:, part] * scale).astype(jnp.bfloat16)
            keys = kvb[:, 0, :, part].reshape(rows, HEAD_DIM)
            values = kvb[:, 1, :, part].reshape(rows, HEAD_DIM)
            scores = lax.dot_general(q, keys, (((1,), (1,)), ((), ())),
                                     preferred_element_type=jnp.float32) * HEAD_DIM ** (-0.5)
            scores = jnp.where(valid, scores, -1e30)
            top = jnp.max(scores, axis=-1, keepdims=True)
            weights = jnp.exp(scores - top)
            norm = jnp.sum(weights, axis=-1, keepdims=True)
            acc = jnp.dot(weights.astype(jnp.bfloat16), values, preferred_element_type=jnp.float32)
            ats[k, :, :, part] = (acc / norm).astype(jnp.bfloat16).reshape(seq, tl, HEAD_DIM)
        peers(lambda d: a_copy(k, d).start())
        atr[k, c, s] = ats[k, s]
        b_copy(k, s).start()

    def finish_chunk(k):
        def one(d):
            a_arrival(k, d).wait_recv()
            b_copy(k, d).start()
        peers(one)
        for d in range(seq):
            b_arrival(k, d).wait_recv()
        for e in range(2):
            for d in range(seq):
                at = (e * seq + d) * cols
                flat[:, at:at + cols] = atr[k, e, d]
        tile = 512
        for j in range(blocks):
            def step(n, carry):
                place = pl.ds(pl.multiple_of(j * width + n * tile, tile), tile)
                acc = jnp.dot(flat[...], woutv[:, place], preferred_element_type=jnp.float32)
                out_ref[k, :, place] = (res[k, :, place].astype(jnp.float32) + acc).astype(jnp.bfloat16)
                return carry
            lax.fori_loop(0, width // tile, step, 0)

            @pl.when(g < segments - 1)
            def _():
                rel_copy(k, j).start()

    def tick(i, carry):
        @pl.when(i < chunks)
        def _():
            send_x(i)

        @pl.when(i == 0)
        def _():
            peers(lambda d: kv_copy(d).start())

        @pl.when(i == 1)
        def _():
            load_wout.wait()

        @pl.when(i > 0)
        def _():
            finish_chunk(i - 1)

        @pl.when(i == 0)
        def _():
            load_wq.wait()

        @pl.when(i < chunks)
        def _():
            collect_x(i)
            project(i)

        @pl.when(i == 0)
        def _():
            load_kv.wait()
            peers(lambda d: kv_arrival(d).wait_recv())

        @pl.when(i < chunks)
        def _():
            attend(i)
        return carry

    lax.fori_loop(0, chunks + 1, tick, 0)

    def drain(k, carry):
        for j in range(blocks):
            @pl.when(blocks * c + j != s)
            def _():
                x_copy(k, j).wait_send()

            @pl.when(g < segments - 1)
            def _():
                rel_copy(k, j).wait_send()

        @pl.when(hub)
        def _():
            for d in range(seq):
                forward_copy(k, d).wait_send()

        def one(d):
            q_copy(k, d).wait_send()
            t_copy(k, d).wait_send()
            a_copy(k, d).wait_send()
        peers(one)
        for d in range(seq):
            b_copy(k, d).wait_send()
        return carry

    lax.fori_loop(0, chunks, drain, 0)
    peers(lambda d: kv_copy(d).wait_send())


def relay(video, caption_kv, caption_lengths, order, gains, w_query, w_out):
    samples, local, half = video.shape
    segments = lax.axis_size("segment")
    seq = lax.axis_size("seq")
    split = SPLIT
    chunks, tl = samples * split, local // split
    tokens = seq * tl
    rows = caption_kv.shape[1]
    width, cols_all = w_query.shape[1:]
    cols = cols_all // seq
    blocks = seq // 2
    ends = jnp.cumsum(caption_lengths)
    bounds = jnp.stack([ends - caption_lengths, ends])[:, order].astype(jnp.int32)
    x0 = jnp.take(video, order, axis=0).reshape(chunks, tl, half)
    kv = caption_kv[0].reshape(rows, 2, seq, cols).transpose(2, 1, 0, 3)
    bf = jnp.bfloat16
    dma = pltpu.SemaphoreType.DMA
    hbm = pl.BlockSpec(memory_space=pl.ANY)
    out = pl.pallas_call(
        functools.partial(relay_kernel, (segments, seq, chunks, tl, split)),
        out_shape=jax.ShapeDtypeStruct((chunks, tl, half), bf),
        in_specs=[pl.BlockSpec(memory_space=pltpu.SMEM), hbm,
                  pl.BlockSpec(memory_space=pltpu.VMEM), hbm, hbm, hbm],
        out_specs=pl.BlockSpec(memory_space=pltpu.VMEM),
        scratch_shapes=[
            pltpu.VMEM((chunks, tl, half), bf),
            pltpu.VMEM((chunks, seq, tl, width), bf),
            pltpu.VMEM((chunks, seq, tokens, cols), bf),
            pltpu.VMEM((chunks, seq, tokens, cols), bf),
            pltpu.VMEM((chunks, 8, tokens), jnp.float32),
            pltpu.VMEM((chunks, seq, 8, tokens), jnp.float32),
            pltpu.VMEM((chunks, seq, tl, cols), bf),
            pltpu.VMEM((chunks, 2, seq, tl, cols), bf),
            pltpu.VMEM((tl, 2 * seq * cols), bf),
            pltpu.VMEM((seq, 2, rows, cols), bf),
            pltpu.VMEM((width, cols_all), bf),
            pltpu.VMEM(w_out.shape[1:], bf),
            dma((4,)), dma((seq,)), dma((seq,)),
            dma((chunks, blocks)), dma((chunks, blocks)),
            dma((chunks, blocks)), dma((chunks, seq)), dma((chunks, seq)),
            dma((chunks, seq)), dma((chunks, seq)), dma((chunks, seq)), dma((chunks, seq)),
            dma((chunks, seq)), dma((chunks, seq)), dma((chunks, seq)), dma((chunks, seq)),
        ],
        compiler_params=pltpu.CompilerParams(
            collective_id=0, has_side_effects=True, vmem_limit_bytes=58 * 2 ** 20),
    )(bounds, x0, gains, kv, w_query[0], w_out[0])
    return out.reshape(1, samples, local, half)


def body(video, caption_kv, caption_lengths, order, gains, w_query, w_out):
    seq = lax.axis_size("seq")
    fits = (
        lax.axis_size("mp") == 2 and seq % 2 == 0
        and w_query.shape[2] % (seq * HEAD_DIM) == 0
        and w_query.shape[1] % 512 == 0
        and (video.shape[1] // SPLIT) % 16 == 0 and caption_kv.shape[1] % 16 == 0
        and (seq * video.shape[1] // SPLIT) % 128 == 0
        and w_out.shape[1] * w_out.shape[2] <= 3072 * 3072
    )
    run = relay if fits else general
    return run(video, caption_kv, caption_lengths, order, gains, w_query, w_out)


def solution(mesh):
    in_specs = (
        P(None, "seq", "mp"),
        P("segment", "seq", None, "mp"),
        P(),
        P(),
        P("segment", None),
        P("segment", "seq", "mp"),
        P("segment", None, "mp"),
    )
    out_specs = P("segment", None, "seq", "mp")
    return jax.shard_map(body, mesh=mesh, in_specs=in_specs, out_specs=out_specs, check_vma=False)
```

```python
import functools
import jax
import jax.numpy as jnp
from jax import lax
from jax.experimental import pallas as pl
from jax.experimental.pallas import tpu as pltpu
from jax.sharding import PartitionSpec as P

HEAD_DIM = 128
SPLIT = 2
MESH = pl.DeviceIdType.MESH


def passed_along(block, axis, distance):
    devices = range(lax.axis_size(axis))
    route = [(i - distance, i) for i in devices if i - distance in devices]
    return lax.ppermute(block, axis, route)


def block_terms(query, kv, start_row, length):
    tokens = query.shape[0]
    heads = query.shape[1] // HEAD_DIM
    count = kv.shape[0]
    qheads = query.reshape(tokens, heads, HEAD_DIM)
    keys = kv[:, 0, :].reshape(count, heads, HEAD_DIM)
    values = kv[:, 1, :].astype(jnp.float32).reshape(count, heads, HEAD_DIM)
    scores = jnp.einsum(
        "thd,rhd->htr", qheads, keys, preferred_element_type=jnp.float32
    ) * HEAD_DIM ** (-0.5)
    rows = jnp.arange(count, dtype=jnp.int32)
    valid = (rows >= start_row) & (rows < start_row + length)
    scores = jnp.where(valid[None, None, :], scores, -1e30)
    top = jnp.max(scores, axis=-1)
    weights = jnp.where(valid[None, None, :], jnp.exp(scores - top[:, :, None]), 0.0)
    total = jnp.sum(weights, axis=-1)
    acc = jnp.einsum("htr,rhd->htd", weights, values)
    return (top, total, acc)


def finish(total, acc):
    heads, tokens, width = acc.shape
    result = acc / total[:, :, None]
    return jnp.transpose(result, (1, 0, 2)).reshape(tokens, heads * width).astype(jnp.bfloat16)


def general(video, caption_kv, caption_lengths, order, gains, w_query, w_out):
    samples = video.shape[0]
    segments = lax.axis_size("segment")
    here = lax.axis_index("segment")
    gain = gains[0]
    w_local = w_query[0]
    out_weight = w_out[0]
    kv_local = caption_kv[0]
    offsets = jnp.cumsum(caption_lengths) - caption_lengths
    w_whole = lax.all_gather(w_local, "seq", axis=0, tiled=True)
    kv_whole = lax.all_gather(kv_local, "seq", axis=0, tiled=True)
    received = jnp.zeros_like(video[0])
    section_out = jnp.zeros_like(video)
    for tick in range(samples + segments - 1):
        micro = tick - here
        active = (micro >= 0) & (micro < samples)
        slot = jnp.clip(micro, 0, samples - 1)
        sample = order[slot]
        first = lax.dynamic_index_in_dim(video, sample, 0, keepdims=False)
        current = jnp.where(here == 0, first, received)
        whole = lax.all_gather(current, "mp", axis=1, tiled=True)
        wholef = whole.astype(jnp.float32)
        meansq = jnp.mean(wholef * wholef, axis=-1, keepdims=True)
        normed = (wholef * lax.rsqrt(meansq + 1e-06) * gain).astype(jnp.bfloat16)
        query = jnp.dot(normed, w_whole, preferred_element_type=jnp.float32)
        query = query.astype(jnp.bfloat16)
        start_row = offsets[sample]
        length = caption_lengths[sample]
        top, total, acc = block_terms(query, kv_whole, start_row, length)
        attended = finish(total, acc)
        projected = jnp.dot(
            lax.all_gather(attended, "mp", axis=1, tiled=True),
            out_weight,
            preferred_element_type=jnp.float32,
        )
        mixed = (current.astype(jnp.float32) + projected).astype(jnp.bfloat16)
        updated = lax.dynamic_update_index_in_dim(section_out, mixed, slot, 0)
        section_out = jnp.where(active, updated, section_out)
        received = passed_along(mixed, "segment", 1)
    return section_out[None]


def relay_kernel(cfg, lengths, order, video_ref, gain_ref, kv_ref, wq_ref, wout_ref, out_ref,
                 res, xg, qs, qr, ts, tr, ats, atr, flat, kvb, wqv, woutv,
                 load_sem, kv_send, kv_recv, rel_send, res_send, res_recv, x_send, x_recv, f_send,
                 q_send, q_recv, t_send, t_recv, a_send, a_recv, b_send, b_recv):
    segments, seq, chunks, tl, split = cfg
    blocks = seq // 2
    g = lax.axis_index("segment")
    s = lax.axis_index("seq")
    c = lax.axis_index("mp")
    width = xg.shape[-1]
    cols = qs.shape[-1]
    half = res.shape[-1]
    tokens = seq * tl
    hub = s // blocks == c
    sibling = {"mp": 1 - c}

    def remote(src, dst, send, recv, device):
        return pltpu.make_async_remote_copy(
            src_ref=src, dst_ref=dst, send_sem=send, recv_sem=recv,
            device_id=device, device_id_type=MESH)

    def peers(fn):
        for off in range(1, seq):
            fn(lax.rem(s + off, seq))

    def kv_copy(d):
        return remote(kv_ref.at[d], kvb.at[s], kv_send.at[d], kv_recv.at[s], {"seq": d})

    def kv_arrival(d):
        return remote(kv_ref.at[d], kvb.at[d], kv_send.at[d], kv_recv.at[d], {"seq": d})

    def next_copy(k, j):
        return remote(out_ref.at[k, :, pl.ds(j * width, width)], xg.at[k, s],
                      rel_send.at[k, j], x_recv.at[k, s], {"segment": g + 1, "seq": blocks * c + j})

    def res_copy(k):
        return remote(out_ref.at[k], res.at[k], res_send.at[k], res_recv.at[k], {"segment": g + 1})

    def res_arrival(k):
        return remote(out_ref.at[k], res.at[k], res_send.at[k], res_recv.at[k], {"segment": g - 1})

    def x_copy(k, j):
        part = pl.ds(j * width, width)
        return remote(res.at[k, :, part], xg.at[k, s], x_send.at[k, j], x_recv.at[k, s],
                      {"seq": blocks * c + j})

    def forward_copy(k, d):
        return remote(xg.at[k, d], xg.at[k, d], f_send.at[k, d], x_recv.at[k, d], sibling)

    def q_copy(k, d):
        return remote(qs.at[k, d], qr.at[k, s], q_send.at[k, d], q_recv.at[k, s], {"seq": d})

    def q_arrival(k, d):
        return remote(qs.at[k, d], qr.at[k, d], q_send.at[k, d], q_recv.at[k, d], {"seq": d})

    def t_copy(k, d):
        return remote(ts.at[k], tr.at[k, s], t_send.at[k, d], t_recv.at[k, s], {"seq": d})

    def t_arrival(k, d):
        return remote(ts.at[k], tr.at[k, d], t_send.at[k, d], t_recv.at[k, d], {"seq": d})

    def a_copy(k, d):
        return remote(ats.at[k, d], atr.at[k, c, s], a_send.at[k, d], a_recv.at[k, s], {"seq": d})

    def a_arrival(k, d):
        return remote(ats.at[k, d], atr.at[k, c, d], a_send.at[k, d], a_recv.at[k, d], {"seq": d})

    def b_copy(k, d):
        return remote(atr.at[k, c, d], atr.at[k, c, d], b_send.at[k, d], b_recv.at[k, d], sibling)

    def b_arrival(k, d):
        return remote(atr.at[k, 1 - c, d], atr.at[k, 1 - c, d], b_send.at[k, d], b_recv.at[k, d], sibling)

    load_wq = pltpu.make_async_copy(wq_ref, wqv, load_sem.at[0])
    load_wout = pltpu.make_async_copy(wout_ref, woutv, load_sem.at[1])
    load_kv = pltpu.make_async_copy(kv_ref.at[s], kvb.at[s], load_sem.at[2])

    load_wq.start()
    load_kv.start()
    load_wout.start()

    barrier = pltpu.get_barrier_semaphore()

    def greet(device):
        pl.semaphore_signal(barrier, inc=1, device_id=device, device_id_type=MESH)

    peers(lambda d: greet({"seq": d}))
    greet(sibling)

    @pl.when((g > 0) & hub)
    def _():
        for d in range(seq):
            greet({"segment": g - 1, "seq": d})

    @pl.when((g > 0) & jnp.logical_not(hub))
    def _():
        greet({"segment": g - 1})

    ahead = g < segments - 1

    @pl.when(jnp.logical_not(ahead))
    def _():
        pl.semaphore_wait(barrier, seq)

    @pl.when(ahead & hub)
    def _():
        pl.semaphore_wait(barrier, seq + blocks)

    @pl.when(ahead & jnp.logical_not(hub))
    def _():
        pl.semaphore_wait(barrier, seq + blocks + 1)

    @pl.when(g == 0)
    def _():
        def choose(k, carry):
            rows = pl.ds(pl.multiple_of(lax.rem(k, split) * tl, tl), tl)
            sample = order[k // split]
            picked = video_ref[0, rows, :]
            for b in range(1, video_ref.shape[0]):
                picked = jnp.where(sample == b, video_ref[b, rows, :], picked)
            res[k] = picked
            return carry
        lax.fori_loop(0, chunks, choose, 0)

    def send_x(k):
        for j in range(blocks):
            mine = blocks * c + j == s

            @pl.when(mine)
            def _():
                xg[k, s] = res[k, :, j * width:(j + 1) * width]
                forward_copy(k, s).start()

            @pl.when(jnp.logical_not(mine))
            def _():
                x_copy(k, j).start()

    def collect_x(k):
        @pl.when(hub)
        def _():
            def one(d):
                forward_copy(k, d).wait_recv()
                forward_copy(k, d).start()
            peers(one)

            @pl.when(g > 0)
            def _():
                one(s)

        @pl.when(jnp.logical_not(hub))
        def _():
            for d in range(seq):
                forward_copy(k, d).wait_recv()

    def project(k):
        x = xg[k].reshape(tokens, width).astype(jnp.float32)
        square = jnp.sum(x * x, axis=-1, keepdims=True)
        ts[k] = jnp.transpose(jnp.broadcast_to(square, (tokens, 128)))[:8]
        y = (x * gain_ref[:, pl.ds(pl.multiple_of(s * width, width), width)]).astype(jnp.bfloat16)

        def one(d):
            t_copy(k, d).start()
            w = wqv[:, pl.ds(pl.multiple_of(d * cols, cols), cols)]
            qs[k, d] = jnp.dot(y, w, preferred_element_type=jnp.float32).astype(jnp.bfloat16)
            q_copy(k, d).start()
        peers(one)
        w = wqv[:, pl.ds(pl.multiple_of(s * cols, cols), cols)]
        qr[k, s] = jnp.dot(y, w, preferred_element_type=jnp.float32).astype(jnp.bfloat16)
        tr[k, s] = ts[k]

    def attend(k):
        def arrived(d):
            t_arrival(k, d).wait_recv()
            q_arrival(k, d).wait_recv()
        peers(arrived)
        square = jnp.sum(tr[k], axis=0)[:1]
        square = jnp.transpose(jnp.broadcast_to(square, (128, tokens)))
        scale = lax.rsqrt(square / (seq * width) + 1e-6)
        total = qr[k, 0].astype(jnp.float32)
        for d in range(1, seq):
            total = total + qr[k, d].astype(jnp.float32)
        micro = k // split
        sample = order[micro]
        first = jnp.int32(0)
        for b in range(video_ref.shape[0] - 1):
            first = first + jnp.where(b < sample, lengths[b], 0)
        last = first + lengths[sample]
        rows = kvb.shape[2] * seq
        index = lax.broadcasted_iota(jnp.int32, (1, rows), 1)
        valid = (index >= first) & (index < last)
        for h in range(cols // HEAD_DIM):
            part = slice(h * HEAD_DIM, (h + 1) * HEAD_DIM)
            q = (total[:, part] * scale).astype(jnp.bfloat16)
            keys = kvb[:, 0, :, part].reshape(rows, HEAD_DIM)
            values = kvb[:, 1, :, part].reshape(rows, HEAD_DIM)
            scores = lax.dot_general(q, keys, (((1,), (1,)), ((), ())),
                                     preferred_element_type=jnp.float32) * HEAD_DIM ** (-0.5)
            scores = jnp.where(valid, scores, -1e30)
            top = jnp.max(scores, axis=-1, keepdims=True)
            weights = jnp.exp(scores - top)
            norm = jnp.sum(weights, axis=-1, keepdims=True)
            acc = jnp.dot(weights.astype(jnp.bfloat16), values, preferred_element_type=jnp.float32)
            ats[k, :, :, part] = (acc / norm).astype(jnp.bfloat16).reshape(seq, tl, HEAD_DIM)
        peers(lambda d: a_copy(k, d).start())
        atr[k, c, s] = ats[k, s]
        b_copy(k, s).start()

    def finish_chunk(k):
        def one(d):
            a_arrival(k, d).wait_recv()
            b_copy(k, d).start()
        peers(one)
        for d in range(seq):
            b_arrival(k, d).wait_recv()
        for e in range(2):
            for d in range(seq):
                at = (e * seq + d) * cols
                flat[:, at:at + cols] = atr[k, e, d]
        tile = 512

        @pl.when(g > 0)
        def _():
            res_arrival(k).wait_recv()

        for j in range(blocks):
            def step(n, carry):
                place = pl.ds(pl.multiple_of(j * width + n * tile, tile), tile)
                acc = jnp.dot(flat[...], woutv[:, place], preferred_element_type=jnp.float32)
                out_ref[k, :, place] = (res[k, :, place].astype(jnp.float32) + acc).astype(jnp.bfloat16)
                return carry
            lax.fori_loop(0, width // tile, step, 0)

            @pl.when(g < segments - 1)
            def _():
                next_copy(k, j).start()

        @pl.when(g < segments - 1)
        def _():
            res_copy(k).start()

    def tick(i, carry):
        @pl.when((i < chunks) & (g == 0))
        def _():
            send_x(i)

        @pl.when(i == 0)
        def _():
            peers(lambda d: kv_copy(d).start())

        @pl.when(i == 0)
        def _():
            load_wq.wait()

        @pl.when(i < chunks)
        def _():
            collect_x(i)
            project(i)

        @pl.when(i == 1)
        def _():
            load_wout.wait()

        @pl.when(i > 0)
        def _():
            finish_chunk(i - 1)

        @pl.when(i == 0)
        def _():
            load_kv.wait()
            peers(lambda d: kv_arrival(d).wait_recv())

        @pl.when(i < chunks)
        def _():
            attend(i)
        return carry

    lax.fori_loop(0, chunks + 1, tick, 0)

    def drain(k, carry):
        for j in range(blocks):
            @pl.when((g == 0) & (blocks * c + j != s))
            def _():
                x_copy(k, j).wait_send()

            @pl.when(g < segments - 1)
            def _():
                next_copy(k, j).wait_send()

        @pl.when(g < segments - 1)
        def _():
            res_copy(k).wait_send()

        @pl.when(hub)
        def _():
            for d in range(seq):
                forward_copy(k, d).wait_send()

        def one(d):
            q_copy(k, d).wait_send()
            t_copy(k, d).wait_send()
            a_copy(k, d).wait_send()
        peers(one)
        for d in range(seq):
            b_copy(k, d).wait_send()
        return carry

    lax.fori_loop(0, chunks, drain, 0)
    peers(lambda d: kv_copy(d).wait_send())


def relay(video, caption_kv, caption_lengths, order, gains, w_query, w_out):
    samples, local, half = video.shape
    segments = lax.axis_size("segment")
    seq = lax.axis_size("seq")
    split = SPLIT
    chunks, tl = samples * split, local // split
    tokens = seq * tl
    rows = caption_kv.shape[1]
    width, cols_all = w_query.shape[1:]
    cols = cols_all // seq
    blocks = seq // 2
    kv = caption_kv[0].reshape(rows, 2, seq, cols).transpose(2, 1, 0, 3)
    bf = jnp.bfloat16
    dma = pltpu.SemaphoreType.DMA
    hbm = pl.BlockSpec(memory_space=pl.ANY)
    vmem = pl.BlockSpec(memory_space=pltpu.VMEM)
    scalars = pl.BlockSpec(memory_space=pltpu.SMEM)
    out = pl.pallas_call(
        functools.partial(relay_kernel, (segments, seq, chunks, tl, split)),
        out_shape=jax.ShapeDtypeStruct((chunks, tl, half), bf),
        in_specs=[scalars, scalars, vmem, vmem, hbm, hbm, hbm],
        out_specs=vmem,
        scratch_shapes=[
            pltpu.VMEM((chunks, tl, half), bf),
            pltpu.VMEM((chunks, seq, tl, width), bf),
            pltpu.VMEM((chunks, seq, tokens, cols), bf),
            pltpu.VMEM((chunks, seq, tokens, cols), bf),
            pltpu.VMEM((chunks, 8, tokens), jnp.float32),
            pltpu.VMEM((chunks, seq, 8, tokens), jnp.float32),
            pltpu.VMEM((chunks, seq, tl, cols), bf),
            pltpu.VMEM((chunks, 2, seq, tl, cols), bf),
            pltpu.VMEM((tl, 2 * seq * cols), bf),
            pltpu.VMEM((seq, 2, rows, cols), bf),
            pltpu.VMEM((width, cols_all), bf),
            pltpu.VMEM(w_out.shape[1:], bf),
            dma((3,)), dma((seq,)), dma((seq,)),
            dma((chunks, blocks)), dma((chunks,)), dma((chunks,)),
            dma((chunks, blocks)), dma((chunks, seq)), dma((chunks, seq)),
            dma((chunks, seq)), dma((chunks, seq)), dma((chunks, seq)), dma((chunks, seq)),
            dma((chunks, seq)), dma((chunks, seq)), dma((chunks, seq)), dma((chunks, seq)),
        ],
        compiler_params=pltpu.CompilerParams(
            collective_id=0, has_side_effects=True, vmem_limit_bytes=58 * 2 ** 20),
    )(caption_lengths, order, video, gains, kv, w_query[0], w_out[0])
    return out.reshape(1, samples, local, half)


def body(video, caption_kv, caption_lengths, order, gains, w_query, w_out):
    seq = lax.axis_size("seq")
    fits = (
        lax.axis_size("mp") == 2 and seq % 2 == 0
        and w_query.shape[2] % (seq * HEAD_DIM) == 0
        and w_query.shape[1] % 512 == 0
        and (video.shape[1] // SPLIT) % 16 == 0 and caption_kv.shape[1] % 16 == 0
        and (seq * video.shape[1] // SPLIT) % 128 == 0
        and w_out.shape[1] * w_out.shape[2] <= 3072 * 3072
    )
    run = relay if fits else general
    return run(video, caption_kv, caption_lengths, order, gains, w_query, w_out)


def solution(mesh):
    in_specs = (
        P(None, "seq", "mp"),
        P("segment", "seq", None, "mp"),
        P(),
        P(),
        P("segment", None),
        P("segment", "seq", "mp"),
        P("segment", None, "mp"),
    )
    out_specs = P("segment", None, "seq", "mp")
    return jax.shard_map(body, mesh=mesh, in_specs=in_specs, out_specs=out_specs, check_vma=False)
```

```python
import functools
import jax
import jax.numpy as jnp
from jax import lax
from jax.experimental import pallas as pl
from jax.experimental.pallas import tpu as pltpu
from jax.sharding import PartitionSpec as P

HEAD_DIM = 128
SPLIT = 2
MESH = pl.DeviceIdType.MESH


def passed_along(block, axis, distance):
    devices = range(lax.axis_size(axis))
    route = [(i - distance, i) for i in devices if i - distance in devices]
    return lax.ppermute(block, axis, route)


def block_terms(query, kv, start_row, length):
    tokens = query.shape[0]
    heads = query.shape[1] // HEAD_DIM
    count = kv.shape[0]
    qheads = query.reshape(tokens, heads, HEAD_DIM)
    keys = kv[:, 0, :].reshape(count, heads, HEAD_DIM)
    values = kv[:, 1, :].astype(jnp.float32).reshape(count, heads, HEAD_DIM)
    scores = jnp.einsum(
        "thd,rhd->htr", qheads, keys, preferred_element_type=jnp.float32
    ) * HEAD_DIM ** (-0.5)
    rows = jnp.arange(count, dtype=jnp.int32)
    valid = (rows >= start_row) & (rows < start_row + length)
    scores = jnp.where(valid[None, None, :], scores, -1e30)
    top = jnp.max(scores, axis=-1)
    weights = jnp.where(valid[None, None, :], jnp.exp(scores - top[:, :, None]), 0.0)
    total = jnp.sum(weights, axis=-1)
    acc = jnp.einsum("htr,rhd->htd", weights, values)
    return (top, total, acc)


def finish(total, acc):
    heads, tokens, width = acc.shape
    result = acc / total[:, :, None]
    return jnp.transpose(result, (1, 0, 2)).reshape(tokens, heads * width).astype(jnp.bfloat16)


def general(video, caption_kv, caption_lengths, order, gains, w_query, w_out):
    samples = video.shape[0]
    segments = lax.axis_size("segment")
    here = lax.axis_index("segment")
    gain = gains[0]
    w_local = w_query[0]
    out_weight = w_out[0]
    kv_local = caption_kv[0]
    offsets = jnp.cumsum(caption_lengths) - caption_lengths
    w_whole = lax.all_gather(w_local, "seq", axis=0, tiled=True)
    kv_whole = lax.all_gather(kv_local, "seq", axis=0, tiled=True)
    received = jnp.zeros_like(video[0])
    section_out = jnp.zeros_like(video)
    for tick in range(samples + segments - 1):
        micro = tick - here
        active = (micro >= 0) & (micro < samples)
        slot = jnp.clip(micro, 0, samples - 1)
        sample = order[slot]
        first = lax.dynamic_index_in_dim(video, sample, 0, keepdims=False)
        current = jnp.where(here == 0, first, received)
        whole = lax.all_gather(current, "mp", axis=1, tiled=True)
        wholef = whole.astype(jnp.float32)
        meansq = jnp.mean(wholef * wholef, axis=-1, keepdims=True)
        normed = (wholef * lax.rsqrt(meansq + 1e-06) * gain).astype(jnp.bfloat16)
        query = jnp.dot(normed, w_whole, preferred_element_type=jnp.float32)
        query = query.astype(jnp.bfloat16)
        start_row = offsets[sample]
        length = caption_lengths[sample]
        top, total, acc = block_terms(query, kv_whole, start_row, length)
        attended = finish(total, acc)
        projected = jnp.dot(
            lax.all_gather(attended, "mp", axis=1, tiled=True),
            out_weight,
            preferred_element_type=jnp.float32,
        )
        mixed = (current.astype(jnp.float32) + projected).astype(jnp.bfloat16)
        updated = lax.dynamic_update_index_in_dim(section_out, mixed, slot, 0)
        section_out = jnp.where(active, updated, section_out)
        received = passed_along(mixed, "segment", 1)
    return section_out[None]


def relay_kernel(cfg, lengths, order, video_ref, gain_ref, kv_ref, wq_ref, wout_ref, out_ref,
                 res, xg, qs, qr, ts, tr, ats, atr, flat, kvb, wqv, woutv,
                 load_sem, kv_send, kv_recv, rel_send, res_send, res_recv, x_send, x_recv, f_send,
                 q_send, q_recv, t_send, t_recv, a_send, a_recv, b_send, b_recv):
    segments, seq, chunks, tl, split = cfg
    blocks = seq // 2
    g = lax.axis_index("segment")
    s = lax.axis_index("seq")
    c = lax.axis_index("mp")
    width = xg.shape[-1]
    cols = qs.shape[-1]
    half = res.shape[-1]
    tokens = seq * tl
    hub = s // blocks == c
    sibling = {"mp": 1 - c}

    def remote(src, dst, send, recv, device):
        return pltpu.make_async_remote_copy(
            src_ref=src, dst_ref=dst, send_sem=send, recv_sem=recv,
            device_id=device, device_id_type=MESH)

    def peers(fn):
        for off in range(1, seq):
            fn(lax.rem(s + off, seq))

    def kv_copy(d):
        return remote(kv_ref.at[d], kvb.at[s], kv_send.at[d], kv_recv.at[s], {"seq": d})

    def kv_arrival(d):
        return remote(kv_ref.at[d], kvb.at[d], kv_send.at[d], kv_recv.at[d], {"seq": d})

    def next_copy(k, j):
        return remote(out_ref.at[k, :, pl.ds(j * width, width)], xg.at[k, s],
                      rel_send.at[k, j], x_recv.at[k, s], {"segment": g + 1, "seq": blocks * c + j})

    def res_copy(k):
        return remote(out_ref.at[k], res.at[k], res_send.at[k], res_recv.at[k], {"segment": g + 1})

    def res_arrival(k):
        return remote(out_ref.at[k], res.at[k], res_send.at[k], res_recv.at[k], {"segment": g - 1})

    def x_copy(k, j):
        part = pl.ds(j * width, width)
        return remote(res.at[k, :, part], xg.at[k, s], x_send.at[k, j], x_recv.at[k, s],
                      {"seq": blocks * c + j})

    def forward_copy(k, d):
        return remote(xg.at[k, d], xg.at[k, d], f_send.at[k, d], x_recv.at[k, d], sibling)

    def q_copy(k, d):
        return remote(qs.at[k, d], qr.at[k, s], q_send.at[k, d], q_recv.at[k, s], {"seq": d})

    def q_arrival(k, d):
        return remote(qs.at[k, d], qr.at[k, d], q_send.at[k, d], q_recv.at[k, d], {"seq": d})

    def t_copy(k, d):
        return remote(ts.at[k], tr.at[k, s], t_send.at[k, d], t_recv.at[k, s], {"seq": d})

    def t_arrival(k, d):
        return remote(ts.at[k], tr.at[k, d], t_send.at[k, d], t_recv.at[k, d], {"seq": d})

    def a_copy(k, d):
        return remote(ats.at[k, d], atr.at[k, c, s], a_send.at[k, d], a_recv.at[k, s], {"seq": d})

    def a_arrival(k, d):
        return remote(ats.at[k, d], atr.at[k, c, d], a_send.at[k, d], a_recv.at[k, d], {"seq": d})

    def b_copy(k, d):
        return remote(atr.at[k, c, d], atr.at[k, c, d], b_send.at[k, d], b_recv.at[k, d], sibling)

    def b_arrival(k, d):
        return remote(atr.at[k, 1 - c, d], atr.at[k, 1 - c, d], b_send.at[k, d], b_recv.at[k, d], sibling)

    load_wq = pltpu.make_async_copy(wq_ref, wqv, load_sem.at[0])
    load_wout = pltpu.make_async_copy(wout_ref, woutv, load_sem.at[1])
    load_kv = pltpu.make_async_copy(kv_ref.at[s], kvb.at[s], load_sem.at[2])

    load_wq.start()
    load_kv.start()
    load_wout.start()

    barrier = pltpu.get_barrier_semaphore()

    def greet(device):
        pl.semaphore_signal(barrier, inc=1, device_id=device, device_id_type=MESH)

    peers(lambda d: greet({"seq": d}))
    greet(sibling)

    @pl.when((g > 0) & hub)
    def _():
        for d in range(seq):
            greet({"segment": g - 1, "seq": d})

    @pl.when((g > 0) & jnp.logical_not(hub))
    def _():
        greet({"segment": g - 1})

    ahead = g < segments - 1

    @pl.when(jnp.logical_not(ahead))
    def _():
        pl.semaphore_wait(barrier, seq)

    @pl.when(ahead & hub)
    def _():
        pl.semaphore_wait(barrier, seq + blocks)

    @pl.when(ahead & jnp.logical_not(hub))
    def _():
        pl.semaphore_wait(barrier, seq + blocks + 1)

    @pl.when(g == 0)
    def _():
        def choose(k, carry):
            rows = pl.ds(pl.multiple_of(lax.rem(k, split) * tl, tl), tl)
            sample = order[k // split]
            picked = video_ref[0, rows, :]
            for b in range(1, video_ref.shape[0]):
                picked = jnp.where(sample == b, video_ref[b, rows, :], picked)
            res[k] = picked
            return carry
        lax.fori_loop(0, chunks, choose, 0)

    def send_x(k):
        for j in range(blocks):
            mine = blocks * c + j == s

            @pl.when(mine)
            def _():
                xg[k, s] = res[k, :, j * width:(j + 1) * width]
                forward_copy(k, s).start()

            @pl.when(jnp.logical_not(mine))
            def _():
                x_copy(k, j).start()

    def collect_x(k):
        @pl.when(hub)
        def _():
            def one(d):
                forward_copy(k, d).wait_recv()
                forward_copy(k, d).start()
            peers(one)

            @pl.when(g > 0)
            def _():
                one(s)

        @pl.when(jnp.logical_not(hub))
        def _():
            for d in range(seq):
                forward_copy(k, d).wait_recv()

    def project(k):
        x = xg[k].reshape(tokens, width).astype(jnp.float32)
        square = jnp.sum(x * x, axis=-1, keepdims=True)
        ts[k] = jnp.transpose(jnp.broadcast_to(square, (tokens, 128)))[:8]
        y = (x * gain_ref[:, pl.ds(pl.multiple_of(s * width, width), width)]).astype(jnp.bfloat16)

        def one(d):
            t_copy(k, d).start()
            w = wqv[:, pl.ds(pl.multiple_of(d * cols, cols), cols)]
            qs[k, d] = jnp.dot(y, w, preferred_element_type=jnp.float32).astype(jnp.bfloat16)
            q_copy(k, d).start()
        peers(one)
        w = wqv[:, pl.ds(pl.multiple_of(s * cols, cols), cols)]
        qr[k, s] = jnp.dot(y, w, preferred_element_type=jnp.float32).astype(jnp.bfloat16)
        tr[k, s] = ts[k]

    def attend(k):
        def arrived(d):
            t_arrival(k, d).wait_recv()
            q_arrival(k, d).wait_recv()
        peers(arrived)
        square = jnp.sum(tr[k], axis=0)[:1]
        square = jnp.transpose(jnp.broadcast_to(square, (128, tokens)))
        scale = lax.rsqrt(square / (seq * width) + 1e-6)
        total = qr[k, 0].astype(jnp.float32)
        for d in range(1, seq):
            total = total + qr[k, d].astype(jnp.float32)
        micro = k // split
        sample = order[micro]
        first = jnp.int32(0)
        for b in range(video_ref.shape[0] - 1):
            first = first + jnp.where(b < sample, lengths[b], 0)
        last = first + lengths[sample]
        rows = kvb.shape[2] * seq
        index = lax.broadcasted_iota(jnp.int32, (1, rows), 1)
        valid = (index >= first) & (index < last)
        for h in range(cols // HEAD_DIM):
            part = slice(h * HEAD_DIM, (h + 1) * HEAD_DIM)
            q = (total[:, part] * scale).astype(jnp.bfloat16)
            keys = kvb[:, 0, :, part].reshape(rows, HEAD_DIM)
            values = kvb[:, 1, :, part].reshape(rows, HEAD_DIM)
            scores = lax.dot_general(q, keys, (((1,), (1,)), ((), ())),
                                     preferred_element_type=jnp.float32) * HEAD_DIM ** (-0.5)
            scores = jnp.where(valid, scores, -1e30)
            top = jnp.max(scores, axis=-1, keepdims=True)
            weights = jnp.exp(scores - top)
            norm = jnp.sum(weights, axis=-1, keepdims=True)
            acc = jnp.dot(weights.astype(jnp.bfloat16), values, preferred_element_type=jnp.float32)
            ats[k, :, :, part] = (acc / norm).astype(jnp.bfloat16).reshape(seq, tl, HEAD_DIM)
        peers(lambda d: a_copy(k, d).start())
        atr[k, c, s] = ats[k, s]
        b_copy(k, s).start()

    def finish_chunk(k):
        def one(d):
            a_arrival(k, d).wait_recv()
            b_copy(k, d).start()
        peers(one)
        for d in range(seq):
            b_arrival(k, d).wait_recv()
        for e in range(2):
            for d in range(seq):
                at = (e * seq + d) * cols
                flat[:, at:at + cols] = atr[k, e, d]
        tile = 512

        @pl.when(g > 0)
        def _():
            res_arrival(k).wait_recv()

        for j in range(blocks):
            def step(n, carry):
                place = pl.ds(pl.multiple_of(j * width + n * tile, tile), tile)
                acc = jnp.dot(flat[...], woutv[:, place], preferred_element_type=jnp.float32)
                out_ref[k, :, place] = (res[k, :, place].astype(jnp.float32) + acc).astype(jnp.bfloat16)
                return carry
            lax.fori_loop(0, width // tile, step, 0)

            @pl.when(g < segments - 1)
            def _():
                next_copy(k, j).start()

        @pl.when(g < segments - 1)
        def _():
            res_copy(k).start()

    def tick(i, carry):
        @pl.when((i == 0) & (g == 0))
        def _():
            send_x(0)

        @pl.when(i == 0)
        def _():
            peers(lambda d: kv_copy(d).start())

        @pl.when(i == 0)
        def _():
            load_wq.wait()

        @pl.when(i < chunks)
        def _():
            collect_x(i)
            project(i)

        @pl.when((i < chunks - 1) & (g == 0))
        def _():
            send_x(i + 1)

        @pl.when(i == 1)
        def _():
            load_wout.wait()

        @pl.when(i > 0)
        def _():
            finish_chunk(i - 1)

        @pl.when(i == 0)
        def _():
            load_kv.wait()
            peers(lambda d: kv_arrival(d).wait_recv())

        @pl.when(i < chunks)
        def _():
            attend(i)
        return carry

    lax.fori_loop(0, chunks + 1, tick, 0)

    def drain(k, carry):
        for j in range(blocks):
            @pl.when((g == 0) & (blocks * c + j != s))
            def _():
                x_copy(k, j).wait_send()

            @pl.when(g < segments - 1)
            def _():
                next_copy(k, j).wait_send()

        @pl.when(g < segments - 1)
        def _():
            res_copy(k).wait_send()

        @pl.when(hub)
        def _():
            for d in range(seq):
                forward_copy(k, d).wait_send()

        def one(d):
            q_copy(k, d).wait_send()
            t_copy(k, d).wait_send()
            a_copy(k, d).wait_send()
        peers(one)
        for d in range(seq):
            b_copy(k, d).wait_send()
        return carry

    lax.fori_loop(0, chunks, drain, 0)
    peers(lambda d: kv_copy(d).wait_send())


def relay(video, caption_kv, caption_lengths, order, gains, w_query, w_out):
    samples, local, half = video.shape
    segments = lax.axis_size("segment")
    seq = lax.axis_size("seq")
    split = SPLIT
    chunks, tl = samples * split, local // split
    tokens = seq * tl
    rows = caption_kv.shape[1]
    width, cols_all = w_query.shape[1:]
    cols = cols_all // seq
    blocks = seq // 2
    kv = caption_kv[0].reshape(rows, 2, seq, cols).transpose(2, 1, 0, 3)
    bf = jnp.bfloat16
    dma = pltpu.SemaphoreType.DMA
    hbm = pl.BlockSpec(memory_space=pl.ANY)
    vmem = pl.BlockSpec(memory_space=pltpu.VMEM)
    scalars = pl.BlockSpec(memory_space=pltpu.SMEM)
    out = pl.pallas_call(
        functools.partial(relay_kernel, (segments, seq, chunks, tl, split)),
        out_shape=jax.ShapeDtypeStruct((chunks, tl, half), bf),
        in_specs=[scalars, scalars, vmem, vmem, hbm, hbm, hbm],
        out_specs=vmem,
        scratch_shapes=[
            pltpu.VMEM((chunks, tl, half), bf),
            pltpu.VMEM((chunks, seq, tl, width), bf),
            pltpu.VMEM((chunks, seq, tokens, cols), bf),
            pltpu.VMEM((chunks, seq, tokens, cols), bf),
            pltpu.VMEM((chunks, 8, tokens), jnp.float32),
            pltpu.VMEM((chunks, seq, 8, tokens), jnp.float32),
            pltpu.VMEM((chunks, seq, tl, cols), bf),
            pltpu.VMEM((chunks, 2, seq, tl, cols), bf),
            pltpu.VMEM((tl, 2 * seq * cols), bf),
            pltpu.VMEM((seq, 2, rows, cols), bf),
            pltpu.VMEM((width, cols_all), bf),
            pltpu.VMEM(w_out.shape[1:], bf),
            dma((3,)), dma((seq,)), dma((seq,)),
            dma((chunks, blocks)), dma((chunks,)), dma((chunks,)),
            dma((chunks, blocks)), dma((chunks, seq)), dma((chunks, seq)),
            dma((chunks, seq)), dma((chunks, seq)), dma((chunks, seq)), dma((chunks, seq)),
            dma((chunks, seq)), dma((chunks, seq)), dma((chunks, seq)), dma((chunks, seq)),
        ],
        compiler_params=pltpu.CompilerParams(
            collective_id=0, has_side_effects=True, vmem_limit_bytes=58 * 2 ** 20),
    )(caption_lengths, order, video, gains, kv, w_query[0], w_out[0])
    return out.reshape(1, samples, local, half)


def body(video, caption_kv, caption_lengths, order, gains, w_query, w_out):
    seq = lax.axis_size("seq")
    fits = (
        lax.axis_size("mp") == 2 and seq % 2 == 0
        and w_query.shape[2] % (seq * HEAD_DIM) == 0
        and w_query.shape[1] % 512 == 0
        and (video.shape[1] // SPLIT) % 16 == 0 and caption_kv.shape[1] % 16 == 0
        and (seq * video.shape[1] // SPLIT) % 128 == 0
        and w_out.shape[1] * w_out.shape[2] <= 3072 * 3072
    )
    run = relay if fits else general
    return run(video, caption_kv, caption_lengths, order, gains, w_query, w_out)


def solution(mesh):
    in_specs = (
        P(None, "seq", "mp"),
        P("segment", "seq", None, "mp"),
        P(),
        P(),
        P("segment", None),
        P("segment", "seq", "mp"),
        P("segment", None, "mp"),
    )
    out_specs = P("segment", None, "seq", "mp")
    return jax.shard_map(body, mesh=mesh, in_specs=in_specs, out_specs=out_specs, check_vma=False)
```

```python
import functools
import jax
import jax.numpy as jnp
from jax import lax
from jax.experimental import pallas as pl
from jax.experimental.pallas import tpu as pltpu
from jax.sharding import PartitionSpec as P

HEAD_DIM = 128
SPLIT = 2
MESH = pl.DeviceIdType.MESH


def passed_along(block, axis, distance):
    devices = range(lax.axis_size(axis))
    route = [(i - distance, i) for i in devices if i - distance in devices]
    return lax.ppermute(block, axis, route)


def block_terms(query, kv, start_row, length):
    tokens = query.shape[0]
    heads = query.shape[1] // HEAD_DIM
    count = kv.shape[0]
    qheads = query.reshape(tokens, heads, HEAD_DIM)
    keys = kv[:, 0, :].reshape(count, heads, HEAD_DIM)
    values = kv[:, 1, :].astype(jnp.float32).reshape(count, heads, HEAD_DIM)
    scores = jnp.einsum(
        "thd,rhd->htr", qheads, keys, preferred_element_type=jnp.float32
    ) * HEAD_DIM ** (-0.5)
    rows = jnp.arange(count, dtype=jnp.int32)
    valid = (rows >= start_row) & (rows < start_row + length)
    scores = jnp.where(valid[None, None, :], scores, -1e30)
    top = jnp.max(scores, axis=-1)
    weights = jnp.where(valid[None, None, :], jnp.exp(scores - top[:, :, None]), 0.0)
    total = jnp.sum(weights, axis=-1)
    acc = jnp.einsum("htr,rhd->htd", weights, values)
    return (top, total, acc)


def finish(total, acc):
    heads, tokens, width = acc.shape
    result = acc / total[:, :, None]
    return jnp.transpose(result, (1, 0, 2)).reshape(tokens, heads * width).astype(jnp.bfloat16)


def general(video, caption_kv, caption_lengths, order, gains, w_query, w_out):
    samples = video.shape[0]
    segments = lax.axis_size("segment")
    here = lax.axis_index("segment")
    gain = gains[0]
    w_local = w_query[0]
    out_weight = w_out[0]
    kv_local = caption_kv[0]
    offsets = jnp.cumsum(caption_lengths) - caption_lengths
    w_whole = lax.all_gather(w_local, "seq", axis=0, tiled=True)
    kv_whole = lax.all_gather(kv_local, "seq", axis=0, tiled=True)
    received = jnp.zeros_like(video[0])
    section_out = jnp.zeros_like(video)
    for tick in range(samples + segments - 1):
        micro = tick - here
        active = (micro >= 0) & (micro < samples)
        slot = jnp.clip(micro, 0, samples - 1)
        sample = order[slot]
        first = lax.dynamic_index_in_dim(video, sample, 0, keepdims=False)
        current = jnp.where(here == 0, first, received)
        whole = lax.all_gather(current, "mp", axis=1, tiled=True)
        wholef = whole.astype(jnp.float32)
        meansq = jnp.mean(wholef * wholef, axis=-1, keepdims=True)
        normed = (wholef * lax.rsqrt(meansq + 1e-06) * gain).astype(jnp.bfloat16)
        query = jnp.dot(normed, w_whole, preferred_element_type=jnp.float32)
        query = query.astype(jnp.bfloat16)
        start_row = offsets[sample]
        length = caption_lengths[sample]
        top, total, acc = block_terms(query, kv_whole, start_row, length)
        attended = finish(total, acc)
        projected = jnp.dot(
            lax.all_gather(attended, "mp", axis=1, tiled=True),
            out_weight,
            preferred_element_type=jnp.float32,
        )
        mixed = (current.astype(jnp.float32) + projected).astype(jnp.bfloat16)
        updated = lax.dynamic_update_index_in_dim(section_out, mixed, slot, 0)
        section_out = jnp.where(active, updated, section_out)
        received = passed_along(mixed, "segment", 1)
    return section_out[None]


def relay_kernel(cfg, lengths, order, video_ref, gain_ref, kv_ref, wq_ref, wout_ref, out_ref,
                 res, xg, qs, qr, ts, tr, ats, atr, flat, kvb, wqv, woutv,
                 load_sem, kv_send, kv_recv, rel_send, res_send, res_recv, x_send, x_recv, f_send,
                 q_send, q_recv, t_send, t_recv, a_send, a_recv, b_send, b_recv):
    segments, seq, chunks, tl, split = cfg
    blocks = seq // 2
    g = lax.axis_index("segment")
    s = lax.axis_index("seq")
    c = lax.axis_index("mp")
    width = xg.shape[-1]
    cols = qs.shape[-1]
    half = res.shape[-1]
    tokens = seq * tl
    hub = s // blocks == c
    sibling = {"mp": 1 - c}

    def remote(src, dst, send, recv, device):
        return pltpu.make_async_remote_copy(
            src_ref=src, dst_ref=dst, send_sem=send, recv_sem=recv,
            device_id=device, device_id_type=MESH)

    def peers(fn):
        for off in range(1, seq):
            fn(lax.rem(s + off, seq))

    def kv_part(d):
        return kv_ref.at[:, :, pl.ds(pl.multiple_of(d * cols, cols), cols)]

    def kv_copy(d):
        return remote(kv_part(d), kvb.at[s], kv_send.at[d], kv_recv.at[s], {"seq": d})

    def kv_arrival(d):
        return remote(kv_part(d), kvb.at[d], kv_send.at[d], kv_recv.at[d], {"seq": d})

    def next_copy(k, j):
        return remote(out_ref.at[k, :, pl.ds(j * width, width)], xg.at[k, s],
                      rel_send.at[k, j], x_recv.at[k, s], {"segment": g + 1, "seq": blocks * c + j})

    def next_tile(k, j, n, tile):
        place = pl.ds(pl.multiple_of(n * tile, tile), tile)
        source = pl.ds(pl.multiple_of(j * width + n * tile, tile), tile)
        return remote(out_ref.at[k, :, source], xg.at[k, s, :, place],
                      rel_send.at[k, j], x_recv.at[k, s], {"segment": g + 1, "seq": blocks * c + j})

    def res_copy(k):
        return remote(out_ref.at[k], res.at[k], res_send.at[k], res_recv.at[k], {"segment": g + 1})

    def res_arrival(k):
        return remote(out_ref.at[k], res.at[k], res_send.at[k], res_recv.at[k], {"segment": g - 1})

    def x_copy(k, j):
        part = pl.ds(j * width, width)
        return remote(res.at[k, :, part], xg.at[k, s], x_send.at[k, j], x_recv.at[k, s],
                      {"seq": blocks * c + j})

    def forward_copy(k, d):
        return remote(xg.at[k, d], xg.at[k, d], f_send.at[k, d], x_recv.at[k, d], sibling)

    def q_copy(k, d):
        return remote(qs.at[k, d], qr.at[k, s], q_send.at[k, d], q_recv.at[k, s], {"seq": d})

    def q_arrival(k, d):
        return remote(qs.at[k, d], qr.at[k, d], q_send.at[k, d], q_recv.at[k, d], {"seq": d})

    def t_copy(k, d):
        return remote(ts.at[k], tr.at[k, s], t_send.at[k, d], t_recv.at[k, s], {"seq": d})

    def t_arrival(k, d):
        return remote(ts.at[k], tr.at[k, d], t_send.at[k, d], t_recv.at[k, d], {"seq": d})

    def a_copy(k, d):
        return remote(ats.at[k, d], atr.at[k, c, s], a_send.at[k, d], a_recv.at[k, s], {"seq": d})

    def a_arrival(k, d):
        return remote(ats.at[k, d], atr.at[k, c, d], a_send.at[k, d], a_recv.at[k, d], {"seq": d})

    def b_copy(k, d):
        return remote(atr.at[k, c, d], atr.at[k, c, d], b_send.at[k, d], b_recv.at[k, d], sibling)

    def b_arrival(k, d):
        return remote(atr.at[k, 1 - c, d], atr.at[k, 1 - c, d], b_send.at[k, d], b_recv.at[k, d], sibling)

    load_wq = pltpu.make_async_copy(wq_ref, wqv, load_sem.at[0])
    load_wout = pltpu.make_async_copy(wout_ref, woutv, load_sem.at[1])
    load_kv = pltpu.make_async_copy(kv_part(s), kvb.at[s], load_sem.at[2])

    load_wq.start()
    load_kv.start()
    load_wout.start()

    barrier = pltpu.get_barrier_semaphore()

    def greet(device):
        pl.semaphore_signal(barrier, inc=1, device_id=device, device_id_type=MESH)

    peers(lambda d: greet({"seq": d}))
    greet(sibling)

    @pl.when((g > 0) & hub)
    def _():
        for d in range(seq):
            greet({"segment": g - 1, "seq": d})

    @pl.when((g > 0) & jnp.logical_not(hub))
    def _():
        greet({"segment": g - 1})

    ahead = g < segments - 1

    @pl.when(jnp.logical_not(ahead))
    def _():
        pl.semaphore_wait(barrier, seq)

    @pl.when(ahead & hub)
    def _():
        pl.semaphore_wait(barrier, seq + blocks)

    @pl.when(ahead & jnp.logical_not(hub))
    def _():
        pl.semaphore_wait(barrier, seq + blocks + 1)

    @pl.when(g == 0)
    def _():
        def choose(k, carry):
            rows = pl.ds(pl.multiple_of(lax.rem(k, split) * tl, tl), tl)
            sample = order[k // split]
            picked = video_ref[0, rows, :]
            for b in range(1, video_ref.shape[0]):
                picked = jnp.where(sample == b, video_ref[b, rows, :], picked)
            res[k] = picked
            return carry
        lax.fori_loop(0, chunks, choose, 0)

    def send_x(k):
        for j in range(blocks):
            mine = blocks * c + j == s

            @pl.when(mine)
            def _():
                xg[k, s] = res[k, :, j * width:(j + 1) * width]
                forward_copy(k, s).start()

            @pl.when(jnp.logical_not(mine))
            def _():
                x_copy(k, j).start()

    def pass_on(k, own):
        def one(d):
            forward_copy(k, d).wait_recv()
            forward_copy(k, d).start()
        peers(one)
        if own:
            one(s)

    def collect_x(k):
        @pl.when(hub & (g > 0))
        def _():
            pass_on(k, True)

        @pl.when(hub & (g == 0) & (k == 0))
        def _():
            pass_on(k, False)

        @pl.when(jnp.logical_not(hub))
        def _():
            for d in range(seq):
                forward_copy(k, d).wait_recv()

    def project(k):
        x = xg[k].reshape(tokens, width).astype(jnp.float32)
        square = jnp.sum(x * x, axis=-1, keepdims=True)
        ts[k] = jnp.transpose(jnp.broadcast_to(square, (tokens, 128)))[:8]
        y = (x * gain_ref[:, pl.ds(pl.multiple_of(s * width, width), width)]).astype(jnp.bfloat16)

        def one(d):
            t_copy(k, d).start()
            w = wqv[:, pl.ds(pl.multiple_of(d * cols, cols), cols)]
            qs[k, d] = jnp.dot(y, w, preferred_element_type=jnp.float32).astype(jnp.bfloat16)
            q_copy(k, d).start()
        peers(one)
        w = wqv[:, pl.ds(pl.multiple_of(s * cols, cols), cols)]
        qr[k, s] = jnp.dot(y, w, preferred_element_type=jnp.float32).astype(jnp.bfloat16)
        tr[k, s] = ts[k]

    def attend(k):
        def arrived(d):
            t_arrival(k, d).wait_recv()
            q_arrival(k, d).wait_recv()
        peers(arrived)
        square = jnp.sum(tr[k], axis=0)[:1]
        square = jnp.transpose(jnp.broadcast_to(square, (128, tokens)))
        scale = lax.rsqrt(square / (seq * width) + 1e-6)
        total = qr[k, 0].astype(jnp.float32)
        for d in range(1, seq):
            total = total + qr[k, d].astype(jnp.float32)
        micro = k // split
        sample = order[micro]
        first = jnp.int32(0)
        for b in range(video_ref.shape[0] - 1):
            first = first + jnp.where(b < sample, lengths[b], 0)
        last = first + lengths[sample]
        rows = kvb.shape[2] * seq
        index = lax.broadcasted_iota(jnp.int32, (1, rows), 1)
        valid = (index >= first) & (index < last)
        for h in range(cols // HEAD_DIM):
            part = slice(h * HEAD_DIM, (h + 1) * HEAD_DIM)
            q = (total[:, part] * scale).astype(jnp.bfloat16)
            keys = kvb[:, 0, :, part].reshape(rows, HEAD_DIM)
            values = kvb[:, 1, :, part].reshape(rows, HEAD_DIM)
            scores = lax.dot_general(q, keys, (((1,), (1,)), ((), ())),
                                     preferred_element_type=jnp.float32) * HEAD_DIM ** (-0.5)
            scores = jnp.where(valid, scores, -1e30)
            top = jnp.max(scores, axis=-1, keepdims=True)
            weights = jnp.exp(scores - top)
            norm = jnp.sum(weights, axis=-1, keepdims=True)
            acc = jnp.dot(weights.astype(jnp.bfloat16), values, preferred_element_type=jnp.float32)
            ats[k, :, :, part] = (acc / norm).astype(jnp.bfloat16).reshape(seq, tl, HEAD_DIM)
        peers(lambda d: a_copy(k, d).start())
        atr[k, c, s] = ats[k, s]
        b_copy(k, s).start()

    def finish_chunk(k):
        def one(d):
            a_arrival(k, d).wait_recv()
            b_copy(k, d).start()
        peers(one)
        for d in range(seq):
            b_arrival(k, d).wait_recv()
        for e in range(2):
            for d in range(seq):
                at = (e * seq + d) * cols
                flat[:, at:at + cols] = atr[k, e, d]
        tile = 512

        @pl.when(g > 0)
        def _():
            res_arrival(k).wait_recv()

        for j in range(blocks):
            def step(n, carry):
                place = pl.ds(pl.multiple_of(j * width + n * tile, tile), tile)
                acc = jnp.dot(flat[...], woutv[:, place], preferred_element_type=jnp.float32)
                out_ref[k, :, place] = (res[k, :, place].astype(jnp.float32) + acc).astype(jnp.bfloat16)

                @pl.when(g < segments - 1)
                def _():
                    next_tile(k, j, n, tile).start()
                return carry
            lax.fori_loop(0, width // tile, step, 0)

        @pl.when(g < segments - 1)
        def _():
            res_copy(k).start()

    def tick(i, carry):
        @pl.when((i == 0) & (g == 0))
        def _():
            send_x(0)

        @pl.when(i == 0)
        def _():
            peers(lambda d: kv_copy(d).start())

        @pl.when((i == 0) & (g == 0))
        def _():
            send_x(1)

        @pl.when(i == 0)
        def _():
            load_wq.wait()

        @pl.when(i < chunks)
        def _():
            collect_x(i)
            project(i)

        @pl.when((i < chunks - 2) & (g == 0))
        def _():
            send_x(i + 2)

        @pl.when(i == 1)
        def _():
            load_wout.wait()

        @pl.when(i > 0)
        def _():
            finish_chunk(i - 1)

        @pl.when(i == 0)
        def _():
            load_kv.wait()
            peers(lambda d: kv_arrival(d).wait_recv())

        @pl.when(i < chunks)
        def _():
            attend(i)

        @pl.when((i < chunks - 1) & (g == 0) & hub)
        def _():
            pass_on(i + 1, False)
        return carry

    lax.fori_loop(0, chunks + 1, tick, 0)

    def drain(k, carry):
        for j in range(blocks):
            @pl.when((g == 0) & (blocks * c + j != s))
            def _():
                x_copy(k, j).wait_send()

            @pl.when(g < segments - 1)
            def _():
                next_copy(k, j).wait_send()

        @pl.when(g < segments - 1)
        def _():
            res_copy(k).wait_send()

        @pl.when(hub)
        def _():
            for d in range(seq):
                forward_copy(k, d).wait_send()

        def one(d):
            q_copy(k, d).wait_send()
            t_copy(k, d).wait_send()
            a_copy(k, d).wait_send()
        peers(one)
        for d in range(seq):
            b_copy(k, d).wait_send()
        return carry

    lax.fori_loop(0, chunks, drain, 0)
    peers(lambda d: kv_copy(d).wait_send())


def relay(video, caption_kv, caption_lengths, order, gains, w_query, w_out):
    samples, local, half = video.shape
    segments = lax.axis_size("segment")
    seq = lax.axis_size("seq")
    split = SPLIT
    chunks, tl = samples * split, local // split
    tokens = seq * tl
    rows = caption_kv.shape[1]
    width, cols_all = w_query.shape[1:]
    cols = cols_all // seq
    blocks = seq // 2
    kv = caption_kv[0].transpose(1, 0, 2)
    bf = jnp.bfloat16
    dma = pltpu.SemaphoreType.DMA
    hbm = pl.BlockSpec(memory_space=pl.ANY)
    vmem = pl.BlockSpec(memory_space=pltpu.VMEM)
    scalars = pl.BlockSpec(memory_space=pltpu.SMEM)
    out = pl.pallas_call(
        functools.partial(relay_kernel, (segments, seq, chunks, tl, split)),
        out_shape=jax.ShapeDtypeStruct((chunks, tl, half), bf),
        in_specs=[scalars, scalars, vmem, vmem, hbm, hbm, hbm],
        out_specs=vmem,
        scratch_shapes=[
            pltpu.VMEM((chunks, tl, half), bf),
            pltpu.VMEM((chunks, seq, tl, width), bf),
            pltpu.VMEM((chunks, seq, tokens, cols), bf),
            pltpu.VMEM((chunks, seq, tokens, cols), bf),
            pltpu.VMEM((chunks, 8, tokens), jnp.float32),
            pltpu.VMEM((chunks, seq, 8, tokens), jnp.float32),
            pltpu.VMEM((chunks, seq, tl, cols), bf),
            pltpu.VMEM((chunks, 2, seq, tl, cols), bf),
            pltpu.VMEM((tl, 2 * seq * cols), bf),
            pltpu.VMEM((seq, 2, rows, cols), bf),
            pltpu.VMEM((width, cols_all), bf),
            pltpu.VMEM(w_out.shape[1:], bf),
            dma((3,)), dma((seq,)), dma((seq,)),
            dma((chunks, blocks)), dma((chunks,)), dma((chunks,)),
            dma((chunks, blocks)), dma((chunks, seq)), dma((chunks, seq)),
            dma((chunks, seq)), dma((chunks, seq)), dma((chunks, seq)), dma((chunks, seq)),
            dma((chunks, seq)), dma((chunks, seq)), dma((chunks, seq)), dma((chunks, seq)),
        ],
        compiler_params=pltpu.CompilerParams(
            collective_id=0, has_side_effects=True, vmem_limit_bytes=58 * 2 ** 20),
    )(caption_lengths, order, video, gains, kv, w_query[0], w_out[0])
    return out.reshape(1, samples, local, half)


def body(video, caption_kv, caption_lengths, order, gains, w_query, w_out):
    seq = lax.axis_size("seq")
    fits = (
        lax.axis_size("mp") == 2 and seq % 2 == 0
        and w_query.shape[2] % (seq * HEAD_DIM) == 0
        and w_query.shape[1] % 512 == 0
        and (video.shape[1] // SPLIT) % 16 == 0 and caption_kv.shape[1] % 16 == 0
        and (seq * video.shape[1] // SPLIT) % 128 == 0
        and w_out.shape[1] * w_out.shape[2] <= 3072 * 3072
    )
    run = relay if fits else general
    return run(video, caption_kv, caption_lengths, order, gains, w_query, w_out)


def solution(mesh):
    in_specs = (
        P(None, "seq", "mp"),
        P("segment", "seq", None, "mp"),
        P(),
        P(),
        P("segment", None),
        P("segment", "seq", "mp"),
        P("segment", None, "mp"),
    )
    out_specs = P("segment", None, "seq", "mp")
    return jax.shard_map(body, mesh=mesh, in_specs=in_specs, out_specs=out_specs, check_vma=False)
```

```python
import functools
import jax
import jax.numpy as jnp
from jax import lax
from jax.experimental import pallas as pl
from jax.experimental.pallas import tpu as pltpu
from jax.sharding import PartitionSpec as P

HEAD_DIM = 128
SPLIT = 2
MESH = pl.DeviceIdType.MESH


def passed_along(block, axis, distance):
    devices = range(lax.axis_size(axis))
    route = [(i - distance, i) for i in devices if i - distance in devices]
    return lax.ppermute(block, axis, route)


def block_terms(query, kv, start_row, length):
    tokens = query.shape[0]
    heads = query.shape[1] // HEAD_DIM
    count = kv.shape[0]
    qheads = query.reshape(tokens, heads, HEAD_DIM)
    keys = kv[:, 0, :].reshape(count, heads, HEAD_DIM)
    values = kv[:, 1, :].astype(jnp.float32).reshape(count, heads, HEAD_DIM)
    scores = jnp.einsum(
        "thd,rhd->htr", qheads, keys, preferred_element_type=jnp.float32
    ) * HEAD_DIM ** (-0.5)
    rows = jnp.arange(count, dtype=jnp.int32)
    valid = (rows >= start_row) & (rows < start_row + length)
    scores = jnp.where(valid[None, None, :], scores, -1e30)
    top = jnp.max(scores, axis=-1)
    weights = jnp.where(valid[None, None, :], jnp.exp(scores - top[:, :, None]), 0.0)
    total = jnp.sum(weights, axis=-1)
    acc = jnp.einsum("htr,rhd->htd", weights, values)
    return (top, total, acc)


def finish(total, acc):
    heads, tokens, width = acc.shape
    result = acc / total[:, :, None]
    return jnp.transpose(result, (1, 0, 2)).reshape(tokens, heads * width).astype(jnp.bfloat16)


def general(video, caption_kv, caption_lengths, order, gains, w_query, w_out):
    samples = video.shape[0]
    segments = lax.axis_size("segment")
    here = lax.axis_index("segment")
    gain = gains[0]
    w_local = w_query[0]
    out_weight = w_out[0]
    kv_local = caption_kv[0]
    offsets = jnp.cumsum(caption_lengths) - caption_lengths
    w_whole = lax.all_gather(w_local, "seq", axis=0, tiled=True)
    kv_whole = lax.all_gather(kv_local, "seq", axis=0, tiled=True)
    received = jnp.zeros_like(video[0])
    section_out = jnp.zeros_like(video)
    for tick in range(samples + segments - 1):
        micro = tick - here
        active = (micro >= 0) & (micro < samples)
        slot = jnp.clip(micro, 0, samples - 1)
        sample = order[slot]
        first = lax.dynamic_index_in_dim(video, sample, 0, keepdims=False)
        current = jnp.where(here == 0, first, received)
        whole = lax.all_gather(current, "mp", axis=1, tiled=True)
        wholef = whole.astype(jnp.float32)
        meansq = jnp.mean(wholef * wholef, axis=-1, keepdims=True)
        normed = (wholef * lax.rsqrt(meansq + 1e-06) * gain).astype(jnp.bfloat16)
        query = jnp.dot(normed, w_whole, preferred_element_type=jnp.float32)
        query = query.astype(jnp.bfloat16)
        start_row = offsets[sample]
        length = caption_lengths[sample]
        top, total, acc = block_terms(query, kv_whole, start_row, length)
        attended = finish(total, acc)
        projected = jnp.dot(
            lax.all_gather(attended, "mp", axis=1, tiled=True),
            out_weight,
            preferred_element_type=jnp.float32,
        )
        mixed = (current.astype(jnp.float32) + projected).astype(jnp.bfloat16)
        updated = lax.dynamic_update_index_in_dim(section_out, mixed, slot, 0)
        section_out = jnp.where(active, updated, section_out)
        received = passed_along(mixed, "segment", 1)
    return section_out[None]


def relay_kernel(cfg, lengths, order, video_ref, gain_ref, kv_ref, wq_ref, wout_ref, out_ref,
                 res, xg, qs, qr, ats, atr, flat, kvb, wqv, woutv,
                 load_sem, kv_send, kv_recv, rel_send, res_send, res_recv, x_send, x_recv, f_send, f_recv,
                 q_send, q_recv, a_send, a_recv, b_send, b_recv):
    segments, seq, chunks, tl, split = cfg
    blocks = seq // 2
    g = lax.axis_index("segment")
    s = lax.axis_index("seq")
    c = lax.axis_index("mp")
    width = xg.shape[-1]
    cols = qs.shape[-1]
    half = res.shape[-1]
    tokens = seq * tl
    hub = s // blocks == c
    sibling = {"mp": 1 - c}

    def remote(src, dst, send, recv, device):
        return pltpu.make_async_remote_copy(
            src_ref=src, dst_ref=dst, send_sem=send, recv_sem=recv,
            device_id=device, device_id_type=MESH)

    def peers(fn):
        for off in range(1, seq):
            fn(lax.rem(s + off, seq))

    def kv_part(d):
        return kv_ref.at[:, :, pl.ds(pl.multiple_of(d * cols, cols), cols)]

    def kv_copy(d):
        return remote(kv_part(d), kvb.at[s], kv_send.at[d], kv_recv.at[s], {"seq": d})

    def kv_arrival(d):
        return remote(kv_part(d), kvb.at[d], kv_send.at[d], kv_recv.at[d], {"seq": d})

    def next_copy(k, j):
        return remote(out_ref.at[k, :, pl.ds(j * width, width)], xg.at[k, s],
                      rel_send.at[k, j], x_recv.at[k, s], {"segment": g + 1, "seq": blocks * c + j})

    def res_copy(k):
        return remote(out_ref.at[k], res.at[k], res_send.at[k], res_recv.at[k], {"segment": g + 1})

    def res_arrival(k):
        return remote(out_ref.at[k], res.at[k], res_send.at[k], res_recv.at[k], {"segment": g - 1})

    def x_copy(k, j):
        part = pl.ds(j * width, width)
        return remote(res.at[k, :, part], xg.at[k, s], x_send.at[k, j], x_recv.at[k, s],
                      {"seq": blocks * c + j})

    def x_arrival(k, d):
        return remote(xg.at[k, d], xg.at[k, d], x_send.at[k, 0], x_recv.at[k, d], {"seq": d})

    def forward_copy(k):
        return remote(xg.at[k], xg.at[k], f_send.at[k], f_recv.at[k], sibling)

    def q_copy(k, d):
        return remote(qs.at[k, d], qr.at[k, s], q_send.at[k, d], q_recv.at[k, s], {"seq": d})

    def q_arrival(k, d):
        return remote(qs.at[k, d], qr.at[k, d], q_send.at[k, d], q_recv.at[k, d], {"seq": d})

    def a_copy(k, d):
        return remote(ats.at[k, d], atr.at[k, c, s], a_send.at[k, d], a_recv.at[k, s], {"seq": d})

    def a_arrival(k, d):
        return remote(ats.at[k, d], atr.at[k, c, d], a_send.at[k, d], a_recv.at[k, d], {"seq": d})

    def b_copy(k):
        return remote(atr.at[k, c], atr.at[k, c], b_send.at[k], b_recv.at[k], sibling)

    def b_arrival(k):
        return remote(atr.at[k, 1 - c], atr.at[k, 1 - c], b_send.at[k], b_recv.at[k], sibling)

    load_wq = pltpu.make_async_copy(wq_ref, wqv, load_sem.at[0])
    load_wout = pltpu.make_async_copy(wout_ref, woutv, load_sem.at[1])
    load_kv = pltpu.make_async_copy(kv_part(s), kvb.at[s], load_sem.at[2])

    load_wq.start()
    load_kv.start()
    load_wout.start()

    barrier = pltpu.get_barrier_semaphore()

    def greet(device):
        pl.semaphore_signal(barrier, inc=1, device_id=device, device_id_type=MESH)

    peers(lambda d: greet({"seq": d}))
    greet(sibling)

    @pl.when((g > 0) & hub)
    def _():
        for d in range(seq):
            greet({"segment": g - 1, "seq": d})

    @pl.when((g > 0) & jnp.logical_not(hub))
    def _():
        greet({"segment": g - 1})

    ahead = g < segments - 1

    @pl.when(jnp.logical_not(ahead))
    def _():
        pl.semaphore_wait(barrier, seq)

    @pl.when(ahead & hub)
    def _():
        pl.semaphore_wait(barrier, seq + blocks)

    @pl.when(ahead & jnp.logical_not(hub))
    def _():
        pl.semaphore_wait(barrier, seq + blocks + 1)

    @pl.when(g == 0)
    def _():
        def choose(k, carry):
            rows = pl.ds(pl.multiple_of(lax.rem(k, split) * tl, tl), tl)
            sample = order[k // split]
            picked = video_ref[0, rows, :]
            for b in range(1, video_ref.shape[0]):
                picked = jnp.where(sample == b, video_ref[b, rows, :], picked)
            res[k] = picked
            return carry
        lax.fori_loop(0, chunks, choose, 0)

    def send_x(k):
        for j in range(blocks):
            mine = blocks * c + j == s

            @pl.when(mine)
            def _():
                xg[k, s] = res[k, :, j * width:(j + 1) * width]

            @pl.when(jnp.logical_not(mine))
            def _():
                x_copy(k, j).start()

    def pass_on(k, own):
        peers(lambda d: x_arrival(k, d).wait_recv())
        if own:
            x_arrival(k, s).wait_recv()
        forward_copy(k).start()

    def collect_x(k):
        @pl.when(hub & (g > 0))
        def _():
            pass_on(k, True)

        @pl.when(hub & (g == 0) & (k == 0))
        def _():
            pass_on(k, False)

        @pl.when(jnp.logical_not(hub))
        def _():
            forward_copy(k).wait_recv()

    def project(k):
        x = xg[k].reshape(tokens, width).astype(jnp.float32)
        square = jnp.sum(x * x, axis=-1, keepdims=True)
        square = jnp.transpose(jnp.broadcast_to(square, (tokens, 128)))[:8]
        high = square.astype(jnp.bfloat16)
        low = (square - high.astype(jnp.float32)).astype(jnp.bfloat16)
        sums = jnp.concatenate([jnp.concatenate([high, low], axis=0)] * (cols // tokens), axis=1)
        y = (x * gain_ref[:, pl.ds(pl.multiple_of(s * width, width), width)]).astype(jnp.bfloat16)

        def one(d):
            w = wqv[:, pl.ds(pl.multiple_of(d * cols, cols), cols)]
            qs[k, d, :tokens] = jnp.dot(y, w, preferred_element_type=jnp.float32).astype(jnp.bfloat16)
            qs[k, d, tokens:] = sums
            q_copy(k, d).start()
        peers(one)
        w = wqv[:, pl.ds(pl.multiple_of(s * cols, cols), cols)]
        qr[k, s, :tokens] = jnp.dot(y, w, preferred_element_type=jnp.float32).astype(jnp.bfloat16)
        qr[k, s, tokens:] = sums

    def attend(k):
        def arrived(d):
            q_arrival(k, d).wait_recv()
        peers(arrived)
        sums = jnp.sum(qr[k, :, tokens:, :tokens].astype(jnp.float32), axis=0)
        square = sums[:1] + sums[8:9]
        square = jnp.transpose(jnp.broadcast_to(square, (128, tokens)))
        scale = lax.rsqrt(square / (seq * width) + 1e-6)
        total = qr[k, 0, :tokens].astype(jnp.float32)
        for d in range(1, seq):
            total = total + qr[k, d, :tokens].astype(jnp.float32)
        micro = k // split
        sample = order[micro]
        first = jnp.int32(0)
        for b in range(video_ref.shape[0] - 1):
            first = first + jnp.where(b < sample, lengths[b], 0)
        last = first + lengths[sample]
        rows = kvb.shape[2] * seq
        index = lax.broadcasted_iota(jnp.int32, (1, rows), 1)
        valid = (index >= first) & (index < last)
        for h in range(cols // HEAD_DIM):
            part = slice(h * HEAD_DIM, (h + 1) * HEAD_DIM)
            q = (total[:, part] * scale).astype(jnp.bfloat16)
            keys = kvb[:, 0, :, part].reshape(rows, HEAD_DIM)
            values = kvb[:, 1, :, part].reshape(rows, HEAD_DIM)
            scores = lax.dot_general(q, keys, (((1,), (1,)), ((), ())),
                                     preferred_element_type=jnp.float32) * HEAD_DIM ** (-0.5)
            scores = jnp.where(valid, scores, -1e30)
            top = jnp.max(scores, axis=-1, keepdims=True)
            weights = jnp.exp(scores - top)
            norm = jnp.sum(weights, axis=-1, keepdims=True)
            acc = jnp.dot(weights.astype(jnp.bfloat16), values, preferred_element_type=jnp.float32)
            ats[k, :, :, part] = (acc / norm).astype(jnp.bfloat16).reshape(seq, tl, HEAD_DIM)
        peers(lambda d: a_copy(k, d).start())
        atr[k, c, s] = ats[k, s]

    def finish_chunk(k):
        peers(lambda d: a_arrival(k, d).wait_recv())
        b_copy(k).start()
        b_arrival(k).wait_recv()
        for e in range(2):
            for d in range(seq):
                at = (e * seq + d) * cols
                flat[:, at:at + cols] = atr[k, e, d]
        tile = 512

        @pl.when(g > 0)
        def _():
            res_arrival(k).wait_recv()

        for j in range(blocks):
            def step(n, carry):
                place = pl.ds(pl.multiple_of(j * width + n * tile, tile), tile)
                acc = jnp.dot(flat[...], woutv[:, place], preferred_element_type=jnp.float32)
                out_ref[k, :, place] = (res[k, :, place].astype(jnp.float32) + acc).astype(jnp.bfloat16)
                return carry
            lax.fori_loop(0, width // tile, step, 0)

            @pl.when(g < segments - 1)
            def _():
                next_copy(k, j).start()

        @pl.when(g < segments - 1)
        def _():
            res_copy(k).start()

    def tick(i, carry):
        @pl.when((i == 0) & (g == 0))
        def _():
            send_x(0)

        @pl.when(i == 0)
        def _():
            peers(lambda d: kv_copy(d).start())

        @pl.when((i == 0) & (g == 0))
        def _():
            send_x(1)

        @pl.when(i == 0)
        def _():
            load_wq.wait()

        @pl.when(i < chunks)
        def _():
            collect_x(i)
            project(i)

        @pl.when((i < chunks - 2) & (g == 0))
        def _():
            send_x(i + 2)

        @pl.when(i == 1)
        def _():
            load_wout.wait()

        @pl.when(i > 0)
        def _():
            finish_chunk(i - 1)

        @pl.when(i == 0)
        def _():
            load_kv.wait()
            peers(lambda d: kv_arrival(d).wait_recv())

        @pl.when(i < chunks)
        def _():
            attend(i)

        @pl.when((i < chunks - 1) & (g == 0) & hub)
        def _():
            pass_on(i + 1, False)
        return carry

    lax.fori_loop(0, chunks + 1, tick, 0)

    def drain(k, carry):
        for j in range(blocks):
            @pl.when((g == 0) & (blocks * c + j != s))
            def _():
                x_copy(k, j).wait_send()

            @pl.when(g < segments - 1)
            def _():
                next_copy(k, j).wait_send()

        @pl.when(g < segments - 1)
        def _():
            res_copy(k).wait_send()

        @pl.when(hub)
        def _():
            forward_copy(k).wait_send()

        def one(d):
            q_copy(k, d).wait_send()
            a_copy(k, d).wait_send()
        peers(one)
        b_copy(k).wait_send()
        return carry

    lax.fori_loop(0, chunks, drain, 0)
    peers(lambda d: kv_copy(d).wait_send())


def relay(video, caption_kv, caption_lengths, order, gains, w_query, w_out):
    samples, local, half = video.shape
    segments = lax.axis_size("segment")
    seq = lax.axis_size("seq")
    split = SPLIT
    chunks, tl = samples * split, local // split
    tokens = seq * tl
    rows = caption_kv.shape[1]
    width, cols_all = w_query.shape[1:]
    cols = cols_all // seq
    blocks = seq // 2
    kv = caption_kv[0].transpose(1, 0, 2)
    bf = jnp.bfloat16
    dma = pltpu.SemaphoreType.DMA
    hbm = pl.BlockSpec(memory_space=pl.ANY)
    vmem = pl.BlockSpec(memory_space=pltpu.VMEM)
    scalars = pl.BlockSpec(memory_space=pltpu.SMEM)
    out = pl.pallas_call(
        functools.partial(relay_kernel, (segments, seq, chunks, tl, split)),
        out_shape=jax.ShapeDtypeStruct((chunks, tl, half), bf),
        in_specs=[scalars, scalars, vmem, vmem, hbm, hbm, hbm],
        out_specs=vmem,
        scratch_shapes=[
            pltpu.VMEM((chunks, tl, half), bf),
            pltpu.VMEM((chunks, seq, tl, width), bf),
            pltpu.VMEM((chunks, seq, tokens + 16, cols), bf),
            pltpu.VMEM((chunks, seq, tokens + 16, cols), bf),
            pltpu.VMEM((chunks, seq, tl, cols), bf),
            pltpu.VMEM((chunks, 2, seq, tl, cols), bf),
            pltpu.VMEM((tl, 2 * seq * cols), bf),
            pltpu.VMEM((seq, 2, rows, cols), bf),
            pltpu.VMEM((width, cols_all), bf),
            pltpu.VMEM(w_out.shape[1:], bf),
            dma((3,)), dma((seq,)), dma((seq,)),
            dma((chunks, blocks)), dma((chunks,)), dma((chunks,)),
            dma((chunks, blocks)), dma((chunks, seq)), dma((chunks,)), dma((chunks,)),
            dma((chunks, seq)), dma((chunks, seq)),
            dma((chunks, seq)), dma((chunks, seq)), dma((chunks,)), dma((chunks,)),
        ],
        compiler_params=pltpu.CompilerParams(
            collective_id=0, has_side_effects=True, vmem_limit_bytes=58 * 2 ** 20),
    )(caption_lengths, order, video, gains, kv, w_query[0], w_out[0])
    return out.reshape(1, samples, local, half)


def body(video, caption_kv, caption_lengths, order, gains, w_query, w_out):
    seq = lax.axis_size("seq")
    fits = (
        lax.axis_size("mp") == 2 and seq % 2 == 0
        and w_query.shape[2] % (seq * HEAD_DIM) == 0
        and w_query.shape[1] % 512 == 0
        and (video.shape[1] // SPLIT) % 16 == 0 and caption_kv.shape[1] % 16 == 0
        and (seq * video.shape[1] // SPLIT) % 128 == 0
        and (w_query.shape[2] // seq) % (seq * video.shape[1] // SPLIT) == 0
        and w_out.shape[1] * w_out.shape[2] <= 3072 * 3072
    )
    run = relay if fits else general
    return run(video, caption_kv, caption_lengths, order, gains, w_query, w_out)


def solution(mesh):
    in_specs = (
        P(None, "seq", "mp"),
        P("segment", "seq", None, "mp"),
        P(),
        P(),
        P("segment", None),
        P("segment", "seq", "mp"),
        P("segment", None, "mp"),
    )
    out_specs = P("segment", None, "seq", "mp")
    return jax.shard_map(body, mesh=mesh, in_specs=in_specs, out_specs=out_specs, check_vma=False)
```

```python
import functools
import jax
import jax.numpy as jnp
from jax import lax
from jax.experimental import pallas as pl
from jax.experimental.pallas import tpu as pltpu
from jax.sharding import PartitionSpec as P

HEAD_DIM = 128
SPLIT = 2
MESH = pl.DeviceIdType.MESH


def passed_along(block, axis, distance):
    devices = range(lax.axis_size(axis))
    route = [(i - distance, i) for i in devices if i - distance in devices]
    return lax.ppermute(block, axis, route)


def block_terms(query, kv, start_row, length):
    tokens = query.shape[0]
    heads = query.shape[1] // HEAD_DIM
    count = kv.shape[0]
    qheads = query.reshape(tokens, heads, HEAD_DIM)
    keys = kv[:, 0, :].reshape(count, heads, HEAD_DIM)
    values = kv[:, 1, :].astype(jnp.float32).reshape(count, heads, HEAD_DIM)
    scores = jnp.einsum(
        "thd,rhd->htr", qheads, keys, preferred_element_type=jnp.float32
    ) * HEAD_DIM ** (-0.5)
    rows = jnp.arange(count, dtype=jnp.int32)
    valid = (rows >= start_row) & (rows < start_row + length)
    scores = jnp.where(valid[None, None, :], scores, -1e30)
    top = jnp.max(scores, axis=-1)
    weights = jnp.where(valid[None, None, :], jnp.exp(scores - top[:, :, None]), 0.0)
    total = jnp.sum(weights, axis=-1)
    acc = jnp.einsum("htr,rhd->htd", weights, values)
    return (top, total, acc)


def finish(total, acc):
    heads, tokens, width = acc.shape
    result = acc / total[:, :, None]
    return jnp.transpose(result, (1, 0, 2)).reshape(tokens, heads * width).astype(jnp.bfloat16)


def general(video, caption_kv, caption_lengths, order, gains, w_query, w_out):
    samples = video.shape[0]
    segments = lax.axis_size("segment")
    here = lax.axis_index("segment")
    gain = gains[0]
    w_local = w_query[0]
    out_weight = w_out[0]
    kv_local = caption_kv[0]
    offsets = jnp.cumsum(caption_lengths) - caption_lengths
    w_whole = lax.all_gather(w_local, "seq", axis=0, tiled=True)
    kv_whole = lax.all_gather(kv_local, "seq", axis=0, tiled=True)
    received = jnp.zeros_like(video[0])
    section_out = jnp.zeros_like(video)
    for tick in range(samples + segments - 1):
        micro = tick - here
        active = (micro >= 0) & (micro < samples)
        slot = jnp.clip(micro, 0, samples - 1)
        sample = order[slot]
        first = lax.dynamic_index_in_dim(video, sample, 0, keepdims=False)
        current = jnp.where(here == 0, first, received)
        whole = lax.all_gather(current, "mp", axis=1, tiled=True)
        wholef = whole.astype(jnp.float32)
        meansq = jnp.mean(wholef * wholef, axis=-1, keepdims=True)
        normed = (wholef * lax.rsqrt(meansq + 1e-06) * gain).astype(jnp.bfloat16)
        query = jnp.dot(normed, w_whole, preferred_element_type=jnp.float32)
        query = query.astype(jnp.bfloat16)
        start_row = offsets[sample]
        length = caption_lengths[sample]
        top, total, acc = block_terms(query, kv_whole, start_row, length)
        attended = finish(total, acc)
        projected = jnp.dot(
            lax.all_gather(attended, "mp", axis=1, tiled=True),
            out_weight,
            preferred_element_type=jnp.float32,
        )
        mixed = (current.astype(jnp.float32) + projected).astype(jnp.bfloat16)
        updated = lax.dynamic_update_index_in_dim(section_out, mixed, slot, 0)
        section_out = jnp.where(active, updated, section_out)
        received = passed_along(mixed, "segment", 1)
    return section_out[None]


def relay_kernel(cfg, lengths, order, video_ref, gain_ref, kv_ref, wq_ref, wout_ref, out_ref,
                 res, xg, qs, qr, ats, atr, flat, kvs, kvb, wqv, woutv,
                 load_sem, stage_sem, kv_send, kv_recv, rel_send, res_send, res_recv, x_send, x_recv, f_send, f_recv,
                 q_send, q_recv, a_send, a_recv, b_send, b_recv):
    segments, seq, chunks, tl, split = cfg
    blocks = seq // 2
    g = lax.axis_index("segment")
    s = lax.axis_index("seq")
    c = lax.axis_index("mp")
    width = xg.shape[-1]
    cols = qs.shape[-1]
    half = res.shape[-1]
    tokens = seq * tl
    hub = s // blocks == c
    sibling = {"mp": 1 - c}

    def remote(src, dst, send, recv, device):
        return pltpu.make_async_remote_copy(
            src_ref=src, dst_ref=dst, send_sem=send, recv_sem=recv,
            device_id=device, device_id_type=MESH)

    def peers(fn):
        for off in range(1, seq):
            fn(lax.rem(s + off, seq))

    def kv_part(d):
        return kv_ref.at[:, :, pl.ds(pl.multiple_of(d * cols, cols), cols)]

    def kv_copy(d):
        return remote(kvs.at[d], kvb.at[s], kv_send.at[d], kv_recv.at[s], {"seq": d})

    def kv_arrival(d):
        return remote(kvs.at[d], kvb.at[d], kv_send.at[d], kv_recv.at[d], {"seq": d})

    def next_copy(k, j):
        return remote(out_ref.at[k, :, pl.ds(j * width, width)], xg.at[k, s],
                      rel_send.at[k, j], x_recv.at[k, s], {"segment": g + 1, "seq": blocks * c + j})

    def res_copy(k):
        return remote(out_ref.at[k], res.at[k], res_send.at[k], res_recv.at[k], {"segment": g + 1})

    def res_arrival(k):
        return remote(out_ref.at[k], res.at[k], res_send.at[k], res_recv.at[k], {"segment": g - 1})

    def x_copy(k, j):
        part = pl.ds(j * width, width)
        return remote(res.at[k, :, part], xg.at[k, s], x_send.at[k, j], x_recv.at[k, s],
                      {"seq": blocks * c + j})

    def x_arrival(k, d):
        return remote(xg.at[k, d], xg.at[k, d], x_send.at[k, 0], x_recv.at[k, d], {"seq": d})

    def forward_copy(k):
        return remote(xg.at[k], xg.at[k], f_send.at[k], f_recv.at[k], sibling)

    def q_copy(k, d):
        return remote(qs.at[k, d], qr.at[k, s], q_send.at[k, d], q_recv.at[k, s], {"seq": d})

    def q_arrival(k, d):
        return remote(qs.at[k, d], qr.at[k, d], q_send.at[k, d], q_recv.at[k, d], {"seq": d})

    def a_copy(k, d):
        return remote(ats.at[k, d], atr.at[k, c, s], a_send.at[k, d], a_recv.at[k, s], {"seq": d})

    def a_arrival(k, d):
        return remote(ats.at[k, d], atr.at[k, c, d], a_send.at[k, d], a_recv.at[k, d], {"seq": d})

    def b_copy(k):
        return remote(atr.at[k, c], atr.at[k, c], b_send.at[k], b_recv.at[k], sibling)

    def b_arrival(k):
        return remote(atr.at[k, 1 - c], atr.at[k, 1 - c], b_send.at[k], b_recv.at[k], sibling)

    load_wq = pltpu.make_async_copy(wq_ref, wqv, load_sem.at[0])
    load_wout = pltpu.make_async_copy(wout_ref, woutv, load_sem.at[1])
    def stage(d):
        return pltpu.make_async_copy(kv_part(d), kvs.at[d], stage_sem.at[d])

    load_kv = pltpu.make_async_copy(kv_part(s), kvb.at[s], load_sem.at[2])

    peers(lambda d: stage(d).start())
    load_kv.start()
    load_wq.start()
    load_wout.start()

    barrier = pltpu.get_barrier_semaphore()

    def greet(device):
        pl.semaphore_signal(barrier, inc=1, device_id=device, device_id_type=MESH)

    peers(lambda d: greet({"seq": d}))
    greet(sibling)

    @pl.when((g > 0) & hub)
    def _():
        for d in range(seq):
            greet({"segment": g - 1, "seq": d})

    @pl.when((g > 0) & jnp.logical_not(hub))
    def _():
        greet({"segment": g - 1})

    ahead = g < segments - 1

    @pl.when(jnp.logical_not(ahead))
    def _():
        pl.semaphore_wait(barrier, seq)

    @pl.when(ahead & hub)
    def _():
        pl.semaphore_wait(barrier, seq + blocks)

    @pl.when(ahead & jnp.logical_not(hub))
    def _():
        pl.semaphore_wait(barrier, seq + blocks + 1)

    @pl.when(g == 0)
    def _():
        def choose(k, carry):
            rows = pl.ds(pl.multiple_of(lax.rem(k, split) * tl, tl), tl)
            sample = order[k // split]
            picked = video_ref[0, rows, :]
            for b in range(1, video_ref.shape[0]):
                picked = jnp.where(sample == b, video_ref[b, rows, :], picked)
            res[k] = picked
            return carry
        lax.fori_loop(0, chunks, choose, 0)

    def send_x(k):
        for j in range(blocks):
            mine = blocks * c + j == s

            @pl.when(mine)
            def _():
                xg[k, s] = res[k, :, j * width:(j + 1) * width]

            @pl.when(jnp.logical_not(mine))
            def _():
                x_copy(k, j).start()

    def pass_on(k, own):
        peers(lambda d: x_arrival(k, d).wait_recv())
        if own:
            x_arrival(k, s).wait_recv()
        forward_copy(k).start()

    def collect_x(k):
        @pl.when(hub & (g > 0))
        def _():
            pass_on(k, True)

        @pl.when(hub & (g == 0) & (k == 0))
        def _():
            pass_on(k, False)

        @pl.when(jnp.logical_not(hub))
        def _():
            forward_copy(k).wait_recv()

    def project(k):
        x = xg[k].reshape(tokens, width).astype(jnp.float32)
        square = jnp.sum(x * x, axis=-1, keepdims=True)
        square = jnp.transpose(jnp.broadcast_to(square, (tokens, 128)))[:8]
        high = square.astype(jnp.bfloat16)
        low = (square - high.astype(jnp.float32)).astype(jnp.bfloat16)
        sums = jnp.concatenate([jnp.concatenate([high, low], axis=0)] * (cols // tokens), axis=1)
        y = (x * gain_ref[:, pl.ds(pl.multiple_of(s * width, width), width)]).astype(jnp.bfloat16)

        def one(d):
            w = wqv[:, pl.ds(pl.multiple_of(d * cols, cols), cols)]
            qs[k, d, :tokens] = jnp.dot(y, w, preferred_element_type=jnp.float32).astype(jnp.bfloat16)
            qs[k, d, tokens:] = sums
            q_copy(k, d).start()
        peers(one)
        w = wqv[:, pl.ds(pl.multiple_of(s * cols, cols), cols)]
        qr[k, s, :tokens] = jnp.dot(y, w, preferred_element_type=jnp.float32).astype(jnp.bfloat16)
        qr[k, s, tokens:] = sums

    def attend(k):
        def arrived(d):
            q_arrival(k, d).wait_recv()
        peers(arrived)
        sums = jnp.sum(qr[k, :, tokens:, :tokens].astype(jnp.float32), axis=0)
        square = sums[:1] + sums[8:9]
        square = jnp.transpose(jnp.broadcast_to(square, (128, tokens)))
        scale = lax.rsqrt(square / (seq * width) + 1e-6)
        total = qr[k, 0, :tokens].astype(jnp.float32)
        for d in range(1, seq):
            total = total + qr[k, d, :tokens].astype(jnp.float32)
        micro = k // split
        sample = order[micro]
        first = jnp.int32(0)
        for b in range(video_ref.shape[0] - 1):
            first = first + jnp.where(b < sample, lengths[b], 0)
        last = first + lengths[sample]
        rows = kvb.shape[2] * seq
        index = lax.broadcasted_iota(jnp.int32, (1, rows), 1)
        valid = (index >= first) & (index < last)
        for h in range(cols // HEAD_DIM):
            part = slice(h * HEAD_DIM, (h + 1) * HEAD_DIM)
            q = (total[:, part] * scale).astype(jnp.bfloat16)
            keys = kvb[:, 0, :, part].reshape(rows, HEAD_DIM)
            values = kvb[:, 1, :, part].reshape(rows, HEAD_DIM)
            scores = lax.dot_general(q, keys, (((1,), (1,)), ((), ())),
                                     preferred_element_type=jnp.float32) * HEAD_DIM ** (-0.5)
            scores = jnp.where(valid, scores, -1e30)
            top = jnp.max(scores, axis=-1, keepdims=True)
            weights = jnp.exp(scores - top)
            norm = jnp.sum(weights, axis=-1, keepdims=True)
            acc = jnp.dot(weights.astype(jnp.bfloat16), values, preferred_element_type=jnp.float32)
            ats[k, :, :, part] = (acc / norm).astype(jnp.bfloat16).reshape(seq, tl, HEAD_DIM)
        peers(lambda d: a_copy(k, d).start())
        atr[k, c, s] = ats[k, s]

    def finish_chunk(k):
        peers(lambda d: a_arrival(k, d).wait_recv())
        b_copy(k).start()
        b_arrival(k).wait_recv()
        for e in range(2):
            for d in range(seq):
                at = (e * seq + d) * cols
                flat[:, at:at + cols] = atr[k, e, d]
        tile = 512

        @pl.when(g > 0)
        def _():
            res_arrival(k).wait_recv()

        for j in range(blocks):
            def step(n, carry):
                place = pl.ds(pl.multiple_of(j * width + n * tile, tile), tile)
                acc = jnp.dot(flat[...], woutv[:, place], preferred_element_type=jnp.float32)
                out_ref[k, :, place] = (res[k, :, place].astype(jnp.float32) + acc).astype(jnp.bfloat16)
                return carry
            lax.fori_loop(0, width // tile, step, 0)

            @pl.when(g < segments - 1)
            def _():
                next_copy(k, j).start()

        @pl.when(g < segments - 1)
        def _():
            res_copy(k).start()

    def tick(i, carry):
        @pl.when((i == 0) & (g == 0))
        def _():
            send_x(0)

        @pl.when(i == 0)
        def _():
            def one(d):
                stage(d).wait()
                kv_copy(d).start()
            peers(one)

        @pl.when(i == 0)
        def _():
            load_wq.wait()

        @pl.when(i < chunks)
        def _():
            collect_x(i)
            project(i)

        @pl.when((i < chunks - 1) & (g == 0))
        def _():
            send_x(i + 1)

        @pl.when(i == 1)
        def _():
            load_wout.wait()

        @pl.when(i > 0)
        def _():
            finish_chunk(i - 1)

        @pl.when(i == 0)
        def _():
            load_kv.wait()
            peers(lambda d: kv_arrival(d).wait_recv())

        @pl.when(i < chunks)
        def _():
            attend(i)

        @pl.when((i < chunks - 1) & (g == 0) & hub)
        def _():
            pass_on(i + 1, False)
        return carry

    lax.fori_loop(0, chunks + 1, tick, 0)

    def drain(k, carry):
        for j in range(blocks):
            @pl.when((g == 0) & (blocks * c + j != s))
            def _():
                x_copy(k, j).wait_send()

            @pl.when(g < segments - 1)
            def _():
                next_copy(k, j).wait_send()

        @pl.when(g < segments - 1)
        def _():
            res_copy(k).wait_send()

        @pl.when(hub)
        def _():
            forward_copy(k).wait_send()

        def one(d):
            q_copy(k, d).wait_send()
            a_copy(k, d).wait_send()
        peers(one)
        b_copy(k).wait_send()
        return carry

    lax.fori_loop(0, chunks, drain, 0)
    peers(lambda d: kv_copy(d).wait_send())


def relay(video, caption_kv, caption_lengths, order, gains, w_query, w_out):
    samples, local, half = video.shape
    segments = lax.axis_size("segment")
    seq = lax.axis_size("seq")
    split = SPLIT
    chunks, tl = samples * split, local // split
    tokens = seq * tl
    rows = caption_kv.shape[1]
    width, cols_all = w_query.shape[1:]
    cols = cols_all // seq
    blocks = seq // 2
    kv = caption_kv[0].transpose(1, 0, 2)
    bf = jnp.bfloat16
    dma = pltpu.SemaphoreType.DMA
    hbm = pl.BlockSpec(memory_space=pl.ANY)
    vmem = pl.BlockSpec(memory_space=pltpu.VMEM)
    scalars = pl.BlockSpec(memory_space=pltpu.SMEM)
    out = pl.pallas_call(
        functools.partial(relay_kernel, (segments, seq, chunks, tl, split)),
        out_shape=jax.ShapeDtypeStruct((chunks, tl, half), bf),
        in_specs=[scalars, scalars, vmem, vmem, hbm, hbm, hbm],
        out_specs=vmem,
        scratch_shapes=[
            pltpu.VMEM((chunks, tl, half), bf),
            pltpu.VMEM((chunks, seq, tl, width), bf),
            pltpu.VMEM((chunks, seq, tokens + 16, cols), bf),
            pltpu.VMEM((chunks, seq, tokens + 16, cols), bf),
            pltpu.VMEM((chunks, seq, tl, cols), bf),
            pltpu.VMEM((chunks, 2, seq, tl, cols), bf),
            pltpu.VMEM((tl, 2 * seq * cols), bf),
            pltpu.VMEM((seq, 2, rows, cols), bf),
            pltpu.VMEM((seq, 2, rows, cols), bf),
            pltpu.VMEM((width, cols_all), bf),
            pltpu.VMEM(w_out.shape[1:], bf),
            dma((3,)), dma((seq,)), dma((seq,)), dma((seq,)),
            dma((chunks, blocks)), dma((chunks,)), dma((chunks,)),
            dma((chunks, blocks)), dma((chunks, seq)), dma((chunks,)), dma((chunks,)),
            dma((chunks, seq)), dma((chunks, seq)),
            dma((chunks, seq)), dma((chunks, seq)), dma((chunks,)), dma((chunks,)),
        ],
        compiler_params=pltpu.CompilerParams(
            collective_id=0, has_side_effects=True, vmem_limit_bytes=58 * 2 ** 20),
    )(caption_lengths, order, video, gains, kv, w_query[0], w_out[0])
    return out.reshape(1, samples, local, half)


def body(video, caption_kv, caption_lengths, order, gains, w_query, w_out):
    seq = lax.axis_size("seq")
    fits = (
        lax.axis_size("mp") == 2 and seq % 2 == 0
        and w_query.shape[2] % (seq * HEAD_DIM) == 0
        and w_query.shape[1] % 512 == 0
        and (video.shape[1] // SPLIT) % 16 == 0 and caption_kv.shape[1] % 16 == 0
        and (seq * video.shape[1] // SPLIT) % 128 == 0
        and (w_query.shape[2] // seq) % (seq * video.shape[1] // SPLIT) == 0
        and w_out.shape[1] * w_out.shape[2] <= 3072 * 3072
    )
    run = relay if fits else general
    return run(video, caption_kv, caption_lengths, order, gains, w_query, w_out)


def solution(mesh):
    in_specs = (
        P(None, "seq", "mp"),
        P("segment", "seq", None, "mp"),
        P(),
        P(),
        P("segment", None),
        P("segment", "seq", "mp"),
        P("segment", None, "mp"),
    )
    out_specs = P("segment", None, "seq", "mp")
    return jax.shard_map(body, mesh=mesh, in_specs=in_specs, out_specs=out_specs, check_vma=False)
```

```python
import functools
import jax
import jax.numpy as jnp
from jax import lax
from jax.experimental import pallas as pl
from jax.experimental.pallas import tpu as pltpu
from jax.sharding import PartitionSpec as P

HEAD_DIM = 128
SPLIT = 2
MESH = pl.DeviceIdType.MESH


def passed_along(block, axis, distance):
    devices = range(lax.axis_size(axis))
    route = [(i - distance, i) for i in devices if i - distance in devices]
    return lax.ppermute(block, axis, route)


def block_terms(query, kv, start_row, length):
    tokens = query.shape[0]
    heads = query.shape[1] // HEAD_DIM
    count = kv.shape[0]
    qheads = query.reshape(tokens, heads, HEAD_DIM)
    keys = kv[:, 0, :].reshape(count, heads, HEAD_DIM)
    values = kv[:, 1, :].astype(jnp.float32).reshape(count, heads, HEAD_DIM)
    scores = jnp.einsum(
        "thd,rhd->htr", qheads, keys, preferred_element_type=jnp.float32
    ) * HEAD_DIM ** (-0.5)
    rows = jnp.arange(count, dtype=jnp.int32)
    valid = (rows >= start_row) & (rows < start_row + length)
    scores = jnp.where(valid[None, None, :], scores, -1e30)
    top = jnp.max(scores, axis=-1)
    weights = jnp.where(valid[None, None, :], jnp.exp(scores - top[:, :, None]), 0.0)
    total = jnp.sum(weights, axis=-1)
    acc = jnp.einsum("htr,rhd->htd", weights, values)
    return (top, total, acc)


def finish(total, acc):
    heads, tokens, width = acc.shape
    result = acc / total[:, :, None]
    return jnp.transpose(result, (1, 0, 2)).reshape(tokens, heads * width).astype(jnp.bfloat16)


def general(video, caption_kv, caption_lengths, order, gains, w_query, w_out):
    samples = video.shape[0]
    segments = lax.axis_size("segment")
    here = lax.axis_index("segment")
    gain = gains[0]
    w_local = w_query[0]
    out_weight = w_out[0]
    kv_local = caption_kv[0]
    offsets = jnp.cumsum(caption_lengths) - caption_lengths
    w_whole = lax.all_gather(w_local, "seq", axis=0, tiled=True)
    kv_whole = lax.all_gather(kv_local, "seq", axis=0, tiled=True)
    received = jnp.zeros_like(video[0])
    section_out = jnp.zeros_like(video)
    for tick in range(samples + segments - 1):
        micro = tick - here
        active = (micro >= 0) & (micro < samples)
        slot = jnp.clip(micro, 0, samples - 1)
        sample = order[slot]
        first = lax.dynamic_index_in_dim(video, sample, 0, keepdims=False)
        current = jnp.where(here == 0, first, received)
        whole = lax.all_gather(current, "mp", axis=1, tiled=True)
        wholef = whole.astype(jnp.float32)
        meansq = jnp.mean(wholef * wholef, axis=-1, keepdims=True)
        normed = (wholef * lax.rsqrt(meansq + 1e-06) * gain).astype(jnp.bfloat16)
        query = jnp.dot(normed, w_whole, preferred_element_type=jnp.float32)
        query = query.astype(jnp.bfloat16)
        start_row = offsets[sample]
        length = caption_lengths[sample]
        top, total, acc = block_terms(query, kv_whole, start_row, length)
        attended = finish(total, acc)
        projected = jnp.dot(
            lax.all_gather(attended, "mp", axis=1, tiled=True),
            out_weight,
            preferred_element_type=jnp.float32,
        )
        mixed = (current.astype(jnp.float32) + projected).astype(jnp.bfloat16)
        updated = lax.dynamic_update_index_in_dim(section_out, mixed, slot, 0)
        section_out = jnp.where(active, updated, section_out)
        received = passed_along(mixed, "segment", 1)
    return section_out[None]


def relay_kernel(cfg, lengths, order, video_ref, gain_ref, kv_ref, wq_ref, wout_ref, out_ref,
                 res, xg, qs, qr, ts, tr, ats, atr, flat, kvs, kvb, wqv, woutv,
                 load_sem, stage_sem, kv_send, kv_recv, rel_send, res_send, res_recv, x_send, x_recv, f_send,
                 q_send, q_recv, t_send, t_recv, a_send, a_recv, b_send, b_recv):
    segments, seq, chunks, tl, split = cfg
    blocks = seq // 2
    g = lax.axis_index("segment")
    s = lax.axis_index("seq")
    c = lax.axis_index("mp")
    width = xg.shape[-1]
    cols = qs.shape[-1]
    half = res.shape[-1]
    tokens = seq * tl
    hub = s // blocks == c
    sibling = {"mp": 1 - c}

    def remote(src, dst, send, recv, device):
        return pltpu.make_async_remote_copy(
            src_ref=src, dst_ref=dst, send_sem=send, recv_sem=recv,
            device_id=device, device_id_type=MESH)

    def peers(fn):
        for off in range(1, seq):
            fn(lax.rem(s + off, seq))

    def kv_part(d):
        return kv_ref.at[:, :, pl.ds(pl.multiple_of(d * cols, cols), cols)]

    def kv_copy(d):
        return remote(kvs.at[d], kvb.at[s], kv_send.at[d], kv_recv.at[s], {"seq": d})

    def kv_arrival(d):
        return remote(kvs.at[d], kvb.at[d], kv_send.at[d], kv_recv.at[d], {"seq": d})

    def next_copy(k, j):
        return remote(out_ref.at[k, :, pl.ds(j * width, width)], xg.at[k, s],
                      rel_send.at[k, j], x_recv.at[k, s], {"segment": g + 1, "seq": blocks * c + j})

    def res_copy(k):
        return remote(out_ref.at[k], res.at[k], res_send.at[k], res_recv.at[k], {"segment": g + 1})

    def res_arrival(k):
        return remote(out_ref.at[k], res.at[k], res_send.at[k], res_recv.at[k], {"segment": g - 1})

    def x_copy(k, j):
        part = pl.ds(j * width, width)
        return remote(res.at[k, :, part], xg.at[k, s], x_send.at[k, j], x_recv.at[k, s],
                      {"seq": blocks * c + j})

    def forward_copy(k, d):
        return remote(xg.at[k, d], xg.at[k, d], f_send.at[k, d], x_recv.at[k, d], sibling)

    def q_copy(k, d):
        return remote(qs.at[k, d], qr.at[k, s], q_send.at[k, d], q_recv.at[k, s], {"seq": d})

    def q_arrival(k, d):
        return remote(qs.at[k, d], qr.at[k, d], q_send.at[k, d], q_recv.at[k, d], {"seq": d})

    def t_copy(k, d):
        return remote(ts.at[k], tr.at[k, s], t_send.at[k, d], t_recv.at[k, s], {"seq": d})

    def t_arrival(k, d):
        return remote(ts.at[k], tr.at[k, d], t_send.at[k, d], t_recv.at[k, d], {"seq": d})

    def a_copy(k, d):
        return remote(ats.at[k, d], atr.at[k, c, s], a_send.at[k, d], a_recv.at[k, s], {"seq": d})

    def a_arrival(k, d):
        return remote(ats.at[k, d], atr.at[k, c, d], a_send.at[k, d], a_recv.at[k, d], {"seq": d})

    def b_copy(k, d):
        return remote(atr.at[k, c, d], atr.at[k, c, d], b_send.at[k, d], b_recv.at[k, d], sibling)

    def b_arrival(k, d):
        return remote(atr.at[k, 1 - c, d], atr.at[k, 1 - c, d], b_send.at[k, d], b_recv.at[k, d], sibling)

    load_wq = pltpu.make_async_copy(wq_ref, wqv, load_sem.at[0])
    load_wout = pltpu.make_async_copy(wout_ref, woutv, load_sem.at[1])
    def stage(d):
        return pltpu.make_async_copy(kv_part(d), kvs.at[d], stage_sem.at[d])

    load_kv = pltpu.make_async_copy(kv_part(s), kvb.at[s], load_sem.at[2])

    peers(lambda d: stage(d).start())
    load_kv.start()
    load_wq.start()
    load_wout.start()

    barrier = pltpu.get_barrier_semaphore()

    def greet(device):
        pl.semaphore_signal(barrier, inc=1, device_id=device, device_id_type=MESH)

    peers(lambda d: greet({"seq": d}))
    greet(sibling)

    @pl.when((g > 0) & hub)
    def _():
        for d in range(seq):
            greet({"segment": g - 1, "seq": d})

    @pl.when((g > 0) & jnp.logical_not(hub))
    def _():
        greet({"segment": g - 1})

    ahead = g < segments - 1

    @pl.when(jnp.logical_not(ahead))
    def _():
        pl.semaphore_wait(barrier, seq)

    @pl.when(ahead & hub)
    def _():
        pl.semaphore_wait(barrier, seq + blocks)

    @pl.when(ahead & jnp.logical_not(hub))
    def _():
        pl.semaphore_wait(barrier, seq + blocks + 1)

    @pl.when(g == 0)
    def _():
        def choose(k, carry):
            rows = pl.ds(pl.multiple_of(lax.rem(k, split) * tl, tl), tl)
            sample = order[k // split]
            picked = video_ref[0, rows, :]
            for b in range(1, video_ref.shape[0]):
                picked = jnp.where(sample == b, video_ref[b, rows, :], picked)
            res[k] = picked
            return carry
        lax.fori_loop(0, chunks, choose, 0)

    def send_x(k):
        for j in range(blocks):
            mine = blocks * c + j == s

            @pl.when(mine)
            def _():
                xg[k, s] = res[k, :, j * width:(j + 1) * width]
                forward_copy(k, s).start()

            @pl.when(jnp.logical_not(mine))
            def _():
                x_copy(k, j).start()

    def pass_on(k, own):
        def one(d):
            forward_copy(k, d).wait_recv()
            forward_copy(k, d).start()
        peers(one)
        if own:
            one(s)

    def collect_x(k):
        @pl.when(hub & (g > 0))
        def _():
            pass_on(k, True)

        @pl.when(hub & (g == 0) & (k == 0))
        def _():
            pass_on(k, False)

        @pl.when(jnp.logical_not(hub))
        def _():
            for d in range(seq):
                forward_copy(k, d).wait_recv()

    def project(k):
        x = xg[k].reshape(tokens, width).astype(jnp.float32)
        square = jnp.sum(x * x, axis=-1, keepdims=True)
        ts[k] = jnp.transpose(jnp.broadcast_to(square, (tokens, 128)))[:8]
        y = (x * gain_ref[:, pl.ds(pl.multiple_of(s * width, width), width)]).astype(jnp.bfloat16)

        def one(d):
            t_copy(k, d).start()
            w = wqv[:, pl.ds(pl.multiple_of(d * cols, cols), cols)]
            qs[k, d] = jnp.dot(y, w, preferred_element_type=jnp.float32).astype(jnp.bfloat16)
            q_copy(k, d).start()
        peers(one)
        w = wqv[:, pl.ds(pl.multiple_of(s * cols, cols), cols)]
        qr[k, s] = jnp.dot(y, w, preferred_element_type=jnp.float32).astype(jnp.bfloat16)
        tr[k, s] = ts[k]

    def attend(k):
        def arrived(d):
            t_arrival(k, d).wait_recv()
            q_arrival(k, d).wait_recv()
        peers(arrived)
        square = jnp.sum(tr[k], axis=0)[:1]
        square = jnp.transpose(jnp.broadcast_to(square, (128, tokens)))
        scale = lax.rsqrt(square / (seq * width) + 1e-6)
        total = qr[k, 0].astype(jnp.float32)
        for d in range(1, seq):
            total = total + qr[k, d].astype(jnp.float32)
        micro = k // split
        sample = order[micro]
        first = jnp.int32(0)
        for b in range(video_ref.shape[0] - 1):
            first = first + jnp.where(b < sample, lengths[b], 0)
        last = first + lengths[sample]
        rows = kvb.shape[2] * seq
        index = lax.broadcasted_iota(jnp.int32, (1, rows), 1)
        valid = (index >= first) & (index < last)
        for h in range(cols // HEAD_DIM):
            part = slice(h * HEAD_DIM, (h + 1) * HEAD_DIM)
            q = (total[:, part] * scale).astype(jnp.bfloat16)
            keys = kvb[:, 0, :, part].reshape(rows, HEAD_DIM)
            values = kvb[:, 1, :, part].reshape(rows, HEAD_DIM)
            scores = lax.dot_general(q, keys, (((1,), (1,)), ((), ())),
                                     preferred_element_type=jnp.float32) * HEAD_DIM ** (-0.5)
            scores = jnp.where(valid, scores, -1e30)
            top = jnp.max(scores, axis=-1, keepdims=True)
            weights = jnp.exp(scores - top)
            norm = jnp.sum(weights, axis=-1, keepdims=True)
            acc = jnp.dot(weights.astype(jnp.bfloat16), values, preferred_element_type=jnp.float32)
            ats[k, :, :, part] = (acc / norm).astype(jnp.bfloat16).reshape(seq, tl, HEAD_DIM)
        peers(lambda d: a_copy(k, d).start())
        atr[k, c, s] = ats[k, s]
        b_copy(k, s).start()

    def finish_chunk(k):
        def one(d):
            a_arrival(k, d).wait_recv()
            b_copy(k, d).start()
        peers(one)
        for d in range(seq):
            b_arrival(k, d).wait_recv()
        for e in range(2):
            for d in range(seq):
                at = (e * seq + d) * cols
                flat[:, at:at + cols] = atr[k, e, d]
        tile = 512

        @pl.when(g > 0)
        def _():
            res_arrival(k).wait_recv()

        for j in range(blocks):
            def step(n, carry):
                place = pl.ds(pl.multiple_of(j * width + n * tile, tile), tile)
                acc = jnp.dot(flat[...], woutv[:, place], preferred_element_type=jnp.float32)
                out_ref[k, :, place] = (res[k, :, place].astype(jnp.float32) + acc).astype(jnp.bfloat16)
                return carry
            lax.fori_loop(0, width // tile, step, 0)

            @pl.when(g < segments - 1)
            def _():
                next_copy(k, j).start()

        @pl.when(g < segments - 1)
        def _():
            res_copy(k).start()

    def tick(i, carry):
        @pl.when((i == 0) & (g == 0))
        def _():
            send_x(0)

        @pl.when(i == 0)
        def _():
            def one(d):
                stage(d).wait()
                kv_copy(d).start()
            peers(one)

        @pl.when(i == 0)
        def _():
            load_wq.wait()

        @pl.when(i < chunks)
        def _():
            collect_x(i)
            project(i)

        @pl.when((i < chunks - 1) & (g == 0))
        def _():
            send_x(i + 1)

        @pl.when(i == 1)
        def _():
            load_wout.wait()

        @pl.when(i > 0)
        def _():
            finish_chunk(i - 1)

        @pl.when(i == 0)
        def _():
            load_kv.wait()
            peers(lambda d: kv_arrival(d).wait_recv())

        @pl.when(i < chunks)
        def _():
            attend(i)

        @pl.when((i < chunks - 1) & (g == 0) & hub)
        def _():
            pass_on(i + 1, False)
        return carry

    lax.fori_loop(0, chunks + 1, tick, 0)

    def drain(k, carry):
        for j in range(blocks):
            @pl.when((g == 0) & (blocks * c + j != s))
            def _():
                x_copy(k, j).wait_send()

            @pl.when(g < segments - 1)
            def _():
                next_copy(k, j).wait_send()

        @pl.when(g < segments - 1)
        def _():
            res_copy(k).wait_send()

        @pl.when(hub)
        def _():
            for d in range(seq):
                forward_copy(k, d).wait_send()

        def one(d):
            q_copy(k, d).wait_send()
            t_copy(k, d).wait_send()
            a_copy(k, d).wait_send()
        peers(one)
        for d in range(seq):
            b_copy(k, d).wait_send()
        return carry

    lax.fori_loop(0, chunks, drain, 0)
    peers(lambda d: kv_copy(d).wait_send())


def relay(video, caption_kv, caption_lengths, order, gains, w_query, w_out):
    samples, local, half = video.shape
    segments = lax.axis_size("segment")
    seq = lax.axis_size("seq")
    split = SPLIT
    chunks, tl = samples * split, local // split
    tokens = seq * tl
    rows = caption_kv.shape[1]
    width, cols_all = w_query.shape[1:]
    cols = cols_all // seq
    blocks = seq // 2
    kv = caption_kv[0].transpose(1, 0, 2)
    bf = jnp.bfloat16
    dma = pltpu.SemaphoreType.DMA
    hbm = pl.BlockSpec(memory_space=pl.ANY)
    vmem = pl.BlockSpec(memory_space=pltpu.VMEM)
    scalars = pl.BlockSpec(memory_space=pltpu.SMEM)
    out = pl.pallas_call(
        functools.partial(relay_kernel, (segments, seq, chunks, tl, split)),
        out_shape=jax.ShapeDtypeStruct((chunks, tl, half), bf),
        in_specs=[scalars, scalars, vmem, vmem, hbm, hbm, hbm],
        out_specs=vmem,
        scratch_shapes=[
            pltpu.VMEM((chunks, tl, half), bf),
            pltpu.VMEM((chunks, seq, tl, width), bf),
            pltpu.VMEM((chunks, seq, tokens, cols), bf),
            pltpu.VMEM((chunks, seq, tokens, cols), bf),
            pltpu.VMEM((chunks, 8, tokens), jnp.float32),
            pltpu.VMEM((chunks, seq, 8, tokens), jnp.float32),
            pltpu.VMEM((chunks, seq, tl, cols), bf),
            pltpu.VMEM((chunks, 2, seq, tl, cols), bf),
            pltpu.VMEM((tl, 2 * seq * cols), bf),
            pltpu.VMEM((seq, 2, rows, cols), bf),
            pltpu.VMEM((seq, 2, rows, cols), bf),
            pltpu.VMEM((width, cols_all), bf),
            pltpu.VMEM(w_out.shape[1:], bf),
            dma((3,)), dma((seq,)), dma((seq,)), dma((seq,)),
            dma((chunks, blocks)), dma((chunks,)), dma((chunks,)),
            dma((chunks, blocks)), dma((chunks, seq)), dma((chunks, seq)),
            dma((chunks, seq)), dma((chunks, seq)), dma((chunks, seq)), dma((chunks, seq)),
            dma((chunks, seq)), dma((chunks, seq)), dma((chunks, seq)), dma((chunks, seq)),
        ],
        compiler_params=pltpu.CompilerParams(
            collective_id=0, has_side_effects=True, vmem_limit_bytes=58 * 2 ** 20),
    )(caption_lengths, order, video, gains, kv, w_query[0], w_out[0])
    return out.reshape(1, samples, local, half)


def body(video, caption_kv, caption_lengths, order, gains, w_query, w_out):
    seq = lax.axis_size("seq")
    fits = (
        lax.axis_size("mp") == 2 and seq % 2 == 0
        and w_query.shape[2] % (seq * HEAD_DIM) == 0
        and w_query.shape[1] % 512 == 0
        and (video.shape[1] // SPLIT) % 16 == 0 and caption_kv.shape[1] % 16 == 0
        and (seq * video.shape[1] // SPLIT) % 128 == 0
        and w_out.shape[1] * w_out.shape[2] <= 3072 * 3072
    )
    run = relay if fits else general
    return run(video, caption_kv, caption_lengths, order, gains, w_query, w_out)


def solution(mesh):
    in_specs = (
        P(None, "seq", "mp"),
        P("segment", "seq", None, "mp"),
        P(),
        P(),
        P("segment", None),
        P("segment", "seq", "mp"),
        P("segment", None, "mp"),
    )
    out_specs = P("segment", None, "seq", "mp")
    return jax.shard_map(body, mesh=mesh, in_specs=in_specs, out_specs=out_specs, check_vma=False)
```

```python
import functools
import jax
import jax.numpy as jnp
from jax import lax
from jax.experimental import pallas as pl
from jax.experimental.pallas import tpu as pltpu
from jax.sharding import PartitionSpec as P

HEAD_DIM = 128
SPLIT = 2
MESH = pl.DeviceIdType.MESH


def passed_along(block, axis, distance):
    devices = range(lax.axis_size(axis))
    route = [(i - distance, i) for i in devices if i - distance in devices]
    return lax.ppermute(block, axis, route)


def block_terms(query, kv, start_row, length):
    tokens = query.shape[0]
    heads = query.shape[1] // HEAD_DIM
    count = kv.shape[0]
    qheads = query.reshape(tokens, heads, HEAD_DIM)
    keys = kv[:, 0, :].reshape(count, heads, HEAD_DIM)
    values = kv[:, 1, :].astype(jnp.float32).reshape(count, heads, HEAD_DIM)
    scores = jnp.einsum(
        "thd,rhd->htr", qheads, keys, preferred_element_type=jnp.float32
    ) * HEAD_DIM ** (-0.5)
    rows = jnp.arange(count, dtype=jnp.int32)
    valid = (rows >= start_row) & (rows < start_row + length)
    scores = jnp.where(valid[None, None, :], scores, -1e30)
    top = jnp.max(scores, axis=-1)
    weights = jnp.where(valid[None, None, :], jnp.exp(scores - top[:, :, None]), 0.0)
    total = jnp.sum(weights, axis=-1)
    acc = jnp.einsum("htr,rhd->htd", weights, values)
    return (top, total, acc)


def finish(total, acc):
    heads, tokens, width = acc.shape
    result = acc / total[:, :, None]
    return jnp.transpose(result, (1, 0, 2)).reshape(tokens, heads * width).astype(jnp.bfloat16)


def general(video, caption_kv, caption_lengths, order, gains, w_query, w_out):
    samples = video.shape[0]
    segments = lax.axis_size("segment")
    here = lax.axis_index("segment")
    gain = gains[0]
    w_local = w_query[0]
    out_weight = w_out[0]
    kv_local = caption_kv[0]
    offsets = jnp.cumsum(caption_lengths) - caption_lengths
    w_whole = lax.all_gather(w_local, "seq", axis=0, tiled=True)
    kv_whole = lax.all_gather(kv_local, "seq", axis=0, tiled=True)
    received = jnp.zeros_like(video[0])
    section_out = jnp.zeros_like(video)
    for tick in range(samples + segments - 1):
        micro = tick - here
        active = (micro >= 0) & (micro < samples)
        slot = jnp.clip(micro, 0, samples - 1)
        sample = order[slot]
        first = lax.dynamic_index_in_dim(video, sample, 0, keepdims=False)
        current = jnp.where(here == 0, first, received)
        whole = lax.all_gather(current, "mp", axis=1, tiled=True)
        wholef = whole.astype(jnp.float32)
        meansq = jnp.mean(wholef * wholef, axis=-1, keepdims=True)
        normed = (wholef * lax.rsqrt(meansq + 1e-06) * gain).astype(jnp.bfloat16)
        query = jnp.dot(normed, w_whole, preferred_element_type=jnp.float32)
        query = query.astype(jnp.bfloat16)
        start_row = offsets[sample]
        length = caption_lengths[sample]
        top, total, acc = block_terms(query, kv_whole, start_row, length)
        attended = finish(total, acc)
        projected = jnp.dot(
            lax.all_gather(attended, "mp", axis=1, tiled=True),
            out_weight,
            preferred_element_type=jnp.float32,
        )
        mixed = (current.astype(jnp.float32) + projected).astype(jnp.bfloat16)
        updated = lax.dynamic_update_index_in_dim(section_out, mixed, slot, 0)
        section_out = jnp.where(active, updated, section_out)
        received = passed_along(mixed, "segment", 1)
    return section_out[None]


def relay_kernel(cfg, lengths, order, video_ref, gain_ref, kv_ref, wq_ref, wout_ref, out_ref,
                 res, xg, qs, qr, ts, tr, ats, atr, flat, kvb, wqv, woutv,
                 load_sem, kv_send, kv_recv, rel_send, res_send, res_recv, x_send, x_recv, f_send,
                 q_send, q_recv, t_send, t_recv, a_send, a_recv, b_send, b_recv):
    segments, seq, chunks, tl, split = cfg
    blocks = seq // 2
    g = lax.axis_index("segment")
    s = lax.axis_index("seq")
    c = lax.axis_index("mp")
    width = xg.shape[-1]
    cols = qs.shape[-1]
    half = res.shape[-1]
    tokens = seq * tl
    hub = s // blocks == c
    sibling = {"mp": 1 - c}

    def remote(src, dst, send, recv, device):
        return pltpu.make_async_remote_copy(
            src_ref=src, dst_ref=dst, send_sem=send, recv_sem=recv,
            device_id=device, device_id_type=MESH)

    def peers(fn):
        for off in range(1, seq):
            fn(lax.rem(s + off, seq))

    def kv_copy(d):
        return remote(kv_ref.at[d], kvb.at[s], kv_send.at[d], kv_recv.at[s], {"seq": d})

    def kv_arrival(d):
        return remote(kv_ref.at[d], kvb.at[d], kv_send.at[d], kv_recv.at[d], {"seq": d})

    def next_copy(k, j):
        return remote(out_ref.at[k, :, pl.ds(j * width, width)], xg.at[k, s],
                      rel_send.at[k, j], x_recv.at[k, s], {"segment": g + 1, "seq": blocks * c + j})

    def res_copy(k):
        return remote(out_ref.at[k], res.at[k], res_send.at[k], res_recv.at[k], {"segment": g + 1})

    def res_arrival(k):
        return remote(out_ref.at[k], res.at[k], res_send.at[k], res_recv.at[k], {"segment": g - 1})

    def x_copy(k, j):
        part = pl.ds(j * width, width)
        return remote(res.at[k, :, part], xg.at[k, s], x_send.at[k, j], x_recv.at[k, s],
                      {"seq": blocks * c + j})

    def forward_copy(k, d):
        return remote(xg.at[k, d], xg.at[k, d], f_send.at[k, d], x_recv.at[k, d], sibling)

    def q_copy(k, d):
        return remote(qs.at[k, d], qr.at[k, s], q_send.at[k, d], q_recv.at[k, s], {"seq": d})

    def q_arrival(k, d):
        return remote(qs.at[k, d], qr.at[k, d], q_send.at[k, d], q_recv.at[k, d], {"seq": d})

    def t_copy(k, d):
        return remote(ts.at[k], tr.at[k, s], t_send.at[k, d], t_recv.at[k, s], {"seq": d})

    def t_arrival(k, d):
        return remote(ts.at[k], tr.at[k, d], t_send.at[k, d], t_recv.at[k, d], {"seq": d})

    def a_copy(k, d):
        return remote(ats.at[k, d], atr.at[k, c, s], a_send.at[k, d], a_recv.at[k, s], {"seq": d})

    def a_arrival(k, d):
        return remote(ats.at[k, d], atr.at[k, c, d], a_send.at[k, d], a_recv.at[k, d], {"seq": d})

    def b_copy(k, d):
        return remote(atr.at[k, c, d], atr.at[k, c, d], b_send.at[k, d], b_recv.at[k, d], sibling)

    def b_arrival(k, d):
        return remote(atr.at[k, 1 - c, d], atr.at[k, 1 - c, d], b_send.at[k, d], b_recv.at[k, d], sibling)

    load_wq = pltpu.make_async_copy(wq_ref, wqv, load_sem.at[0])
    load_wout = pltpu.make_async_copy(wout_ref, woutv, load_sem.at[1])
    load_kv = pltpu.make_async_copy(kv_ref.at[s], kvb.at[s], load_sem.at[2])

    load_wq.start()
    load_kv.start()
    load_wout.start()

    barrier = pltpu.get_barrier_semaphore()

    def greet(device):
        pl.semaphore_signal(barrier, inc=1, device_id=device, device_id_type=MESH)

    peers(lambda d: greet({"seq": d}))
    greet(sibling)

    @pl.when((g > 0) & hub)
    def _():
        for d in range(seq):
            greet({"segment": g - 1, "seq": d})

    @pl.when((g > 0) & jnp.logical_not(hub))
    def _():
        greet({"segment": g - 1})

    ahead = g < segments - 1

    @pl.when(jnp.logical_not(ahead))
    def _():
        pl.semaphore_wait(barrier, seq)

    @pl.when(ahead & hub)
    def _():
        pl.semaphore_wait(barrier, seq + blocks)

    @pl.when(ahead & jnp.logical_not(hub))
    def _():
        pl.semaphore_wait(barrier, seq + blocks + 1)

    @pl.when(g == 0)
    def _():
        def choose(k, carry):
            rows = pl.ds(pl.multiple_of(lax.rem(k, split) * tl, tl), tl)
            sample = order[k // split]
            picked = video_ref[0, rows, :]
            for b in range(1, video_ref.shape[0]):
                picked = jnp.where(sample == b, video_ref[b, rows, :], picked)
            res[k] = picked
            return carry
        lax.fori_loop(0, chunks, choose, 0)

    def send_x(k):
        for j in range(blocks):
            mine = blocks * c + j == s

            @pl.when(mine)
            def _():
                xg[k, s] = res[k, :, j * width:(j + 1) * width]
                forward_copy(k, s).start()

            @pl.when(jnp.logical_not(mine))
            def _():
                x_copy(k, j).start()

    def collect_x(k):
        @pl.when(hub)
        def _():
            def one(d):
                forward_copy(k, d).wait_recv()
                forward_copy(k, d).start()
            peers(one)

            @pl.when(g > 0)
            def _():
                one(s)

        @pl.when(jnp.logical_not(hub))
        def _():
            for d in range(seq):
                forward_copy(k, d).wait_recv()

    def project(k):
        x = xg[k].reshape(tokens, width).astype(jnp.float32)
        square = jnp.sum(x * x, axis=-1, keepdims=True)
        ts[k] = jnp.transpose(jnp.broadcast_to(square, (tokens, 128)))[:8]
        y = (x * gain_ref[:, pl.ds(pl.multiple_of(s * width, width), width)]).astype(jnp.bfloat16)

        peers(lambda d: t_copy(k, d).start())
        pairs = seq // 2
        for turn in range(1, pairs + 1):
            pair = lax.rem(s // 2 + turn, pairs)
            w = wqv[:, pl.ds(pl.multiple_of(pair * 2 * cols, 2 * cols), 2 * cols)]
            both = jnp.dot(y, w, preferred_element_type=jnp.float32).astype(jnp.bfloat16)
            for e in range(2):
                d = 2 * pair + e
                block = both[:, e * cols:(e + 1) * cols]
                if turn < pairs:
                    qs[k, d] = block
                    q_copy(k, d).start()
                    continue

                @pl.when(d == s)
                def _():
                    qr[k, s] = block

                @pl.when(d != s)
                def _():
                    qs[k, d] = block
                    q_copy(k, d).start()
        tr[k, s] = ts[k]

    def attend(k):
        def arrived(d):
            t_arrival(k, d).wait_recv()
            q_arrival(k, d).wait_recv()
        peers(arrived)
        square = jnp.sum(tr[k], axis=0)[:1]
        square = jnp.transpose(jnp.broadcast_to(square, (128, tokens)))
        scale = lax.rsqrt(square / (seq * width) + 1e-6)
        total = qr[k, 0].astype(jnp.float32)
        for d in range(1, seq):
            total = total + qr[k, d].astype(jnp.float32)
        micro = k // split
        sample = order[micro]
        first = jnp.int32(0)
        for b in range(video_ref.shape[0] - 1):
            first = first + jnp.where(b < sample, lengths[b], 0)
        last = first + lengths[sample]
        rows = kvb.shape[2] * seq
        index = lax.broadcasted_iota(jnp.int32, (1, rows), 1)
        valid = (index >= first) & (index < last)
        for h in range(cols // HEAD_DIM):
            part = slice(h * HEAD_DIM, (h + 1) * HEAD_DIM)
            q = (total[:, part] * scale).astype(jnp.bfloat16)
            keys = kvb[:, 0, :, part].reshape(rows, HEAD_DIM)
            values = kvb[:, 1, :, part].reshape(rows, HEAD_DIM)
            scores = lax.dot_general(q, keys, (((1,), (1,)), ((), ())),
                                     preferred_element_type=jnp.float32) * HEAD_DIM ** (-0.5)
            scores = jnp.where(valid, scores, -1e30)
            top = jnp.max(scores, axis=-1, keepdims=True)
            weights = jnp.exp(scores - top)
            norm = jnp.sum(weights, axis=-1, keepdims=True)
            acc = jnp.dot(weights.astype(jnp.bfloat16), values, preferred_element_type=jnp.float32)
            ats[k, :, :, part] = (acc / norm).astype(jnp.bfloat16).reshape(seq, tl, HEAD_DIM)
        peers(lambda d: a_copy(k, d).start())
        atr[k, c, s] = ats[k, s]
        b_copy(k, s).start()

    def finish_chunk(k):
        def one(d):
            a_arrival(k, d).wait_recv()
            b_copy(k, d).start()
        peers(one)
        for d in range(seq):
            b_arrival(k, d).wait_recv()
        for e in range(2):
            for d in range(seq):
                at = (e * seq + d) * cols
                flat[:, at:at + cols] = atr[k, e, d]
        tile = 768 if width % 768 == 0 else 512

        @pl.when(g > 0)
        def _():
            res_arrival(k).wait_recv()

        for j in range(blocks):
            def step(n, carry):
                place = pl.ds(pl.multiple_of(j * width + n * tile, tile), tile)
                acc = jnp.dot(flat[...], woutv[:, place], preferred_element_type=jnp.float32)
                out_ref[k, :, place] = (res[k, :, place].astype(jnp.float32) + acc).astype(jnp.bfloat16)
                return carry
            lax.fori_loop(0, width // tile, step, 0)

            @pl.when(g < segments - 1)
            def _():
                next_copy(k, j).start()

        @pl.when(g < segments - 1)
        def _():
            res_copy(k).start()

    def tick(i, carry):
        @pl.when((i == 0) & (g == 0))
        def _():
            send_x(0)

        @pl.when(i == 0)
        def _():
            peers(lambda d: kv_copy(d).start())

        @pl.when(i == 0)
        def _():
            load_wq.wait()

        @pl.when(i < chunks)
        def _():
            collect_x(i)
            project(i)

        @pl.when((i < chunks - 1) & (g == 0))
        def _():
            send_x(i + 1)

        @pl.when(i == 1)
        def _():
            load_wout.wait()

        @pl.when(i > 0)
        def _():
            finish_chunk(i - 1)

        @pl.when(i == 0)
        def _():
            load_kv.wait()
            peers(lambda d: kv_arrival(d).wait_recv())

        @pl.when(i < chunks)
        def _():
            attend(i)
        return carry

    lax.fori_loop(0, chunks + 1, tick, 0)

    def drain(k, carry):
        for j in range(blocks):
            @pl.when((g == 0) & (blocks * c + j != s))
            def _():
                x_copy(k, j).wait_send()

            @pl.when(g < segments - 1)
            def _():
                next_copy(k, j).wait_send()

        @pl.when(g < segments - 1)
        def _():
            res_copy(k).wait_send()

        @pl.when(hub)
        def _():
            for d in range(seq):
                forward_copy(k, d).wait_send()

        def one(d):
            q_copy(k, d).wait_send()
            t_copy(k, d).wait_send()
            a_copy(k, d).wait_send()
        peers(one)
        for d in range(seq):
            b_copy(k, d).wait_send()
        return carry

    lax.fori_loop(0, chunks, drain, 0)
    peers(lambda d: kv_copy(d).wait_send())


def relay(video, caption_kv, caption_lengths, order, gains, w_query, w_out):
    samples, local, half = video.shape
    segments = lax.axis_size("segment")
    seq = lax.axis_size("seq")
    split = SPLIT
    chunks, tl = samples * split, local // split
    tokens = seq * tl
    rows = caption_kv.shape[1]
    width, cols_all = w_query.shape[1:]
    cols = cols_all // seq
    blocks = seq // 2
    kv = caption_kv[0].reshape(rows, 2, seq, cols).transpose(2, 1, 0, 3)
    bf = jnp.bfloat16
    dma = pltpu.SemaphoreType.DMA
    hbm = pl.BlockSpec(memory_space=pl.ANY)
    vmem = pl.BlockSpec(memory_space=pltpu.VMEM)
    scalars = pl.BlockSpec(memory_space=pltpu.SMEM)
    out = pl.pallas_call(
        functools.partial(relay_kernel, (segments, seq, chunks, tl, split)),
        out_shape=jax.ShapeDtypeStruct((chunks, tl, half), bf),
        in_specs=[scalars, scalars, vmem, vmem, hbm, hbm, hbm],
        out_specs=vmem,
        scratch_shapes=[
            pltpu.VMEM((chunks, tl, half), bf),
            pltpu.VMEM((chunks, seq, tl, width), bf),
            pltpu.VMEM((chunks, seq, tokens, cols), bf),
            pltpu.VMEM((chunks, seq, tokens, cols), bf),
            pltpu.VMEM((chunks, 8, tokens), jnp.float32),
            pltpu.VMEM((chunks, seq, 8, tokens), jnp.float32),
            pltpu.VMEM((chunks, seq, tl, cols), bf),
            pltpu.VMEM((chunks, 2, seq, tl, cols), bf),
            pltpu.VMEM((tl, 2 * seq * cols), bf),
            pltpu.VMEM((seq, 2, rows, cols), bf),
            pltpu.VMEM((width, cols_all), bf),
            pltpu.VMEM(w_out.shape[1:], bf),
            dma((3,)), dma((seq,)), dma((seq,)),
            dma((chunks, blocks)), dma((chunks,)), dma((chunks,)),
            dma((chunks, blocks)), dma((chunks, seq)), dma((chunks, seq)),
            dma((chunks, seq)), dma((chunks, seq)), dma((chunks, seq)), dma((chunks, seq)),
            dma((chunks, seq)), dma((chunks, seq)), dma((chunks, seq)), dma((chunks, seq)),
        ],
        compiler_params=pltpu.CompilerParams(
            collective_id=0, has_side_effects=True, vmem_limit_bytes=58 * 2 ** 20),
    )(caption_lengths, order, video, gains, kv, w_query[0], w_out[0])
    return out.reshape(1, samples, local, half)


def body(video, caption_kv, caption_lengths, order, gains, w_query, w_out):
    seq = lax.axis_size("seq")
    fits = (
        lax.axis_size("mp") == 2 and seq % 2 == 0
        and w_query.shape[2] % (seq * HEAD_DIM) == 0
        and w_query.shape[1] % 512 == 0
        and (video.shape[1] // SPLIT) % 16 == 0 and caption_kv.shape[1] % 16 == 0
        and (seq * video.shape[1] // SPLIT) % 128 == 0
        and w_out.shape[1] * w_out.shape[2] <= 3072 * 3072
    )
    run = relay if fits else general
    return run(video, caption_kv, caption_lengths, order, gains, w_query, w_out)


def solution(mesh):
    in_specs = (
        P(None, "seq", "mp"),
        P("segment", "seq", None, "mp"),
        P(),
        P(),
        P("segment", None),
        P("segment", "seq", "mp"),
        P("segment", None, "mp"),
    )
    out_specs = P("segment", None, "seq", "mp")
    return jax.shard_map(body, mesh=mesh, in_specs=in_specs, out_specs=out_specs, check_vma=False)
```
